128 devices in a mesh: dp: 4 (over y), expert: 32 (over x, z, core).
Axes of the slice: x: 4, y: 4, z: 4, core: 2. Of those that a mesh axis runs over, the one named last changes fastest.
Arguments:
- hidden_rows: bfloat16 [3072, 7168], P(('dp', 'expert')), may hold values from -6 to 6
- expert_ids: int32 [3072, 8], P(('dp', 'expert')), may hold values from 0 to 63, all different within a row; in each aligned block of 24 rows (0 to 23, 24 to 47, ...) at most 4 rows name the same one
- gate_weights: float32 [3072, 8], P(('dp', 'expert')), may hold values from 0.05 to 0.5
- gate_matrix: bfloat16 [64, 7168, 1024], P('expert', None, 'dp'), may hold values from -0.0625 to 0.0625
- up_matrix: bfloat16 [64, 7168, 1024], P('expert', None, 'dp'), may hold values from -0.0625 to 0.0625
- down_matrix: bfloat16 [64, 1024, 7168], P('expert', 'dp'), may hold values from -0.1875 to 0.1875
- module_gain: float32 [7168], replicated, may hold values from 0.5 to 1.5
- accepted: int32 [1024], P(('dp', 'expert')), may hold values from 0 to 2
- owner_map: int32 [1024], P(('dp', 'expert')), may hold values from 0 to 31, as said below
Outputs:
- final_rows: bfloat16 [3072, 7168], P(('dp', 'expert'))
- module_rows: bfloat16 [4, 32, 32, 6, 7168], P('dp', 'expert')
The draws below stay inside these ranges and needn't reach their ends.
Inputs may be any that keep to these rules, and one draw needn't show every extreme that they name: `expert_ids`: within the 24 rows of one device no expert is named more than 4 times, a bound that some block reaches. `owner_map`: the requests of one device name one owner at most twice. In each group of devices along expert, one owner is named by two requests of every device of the group, and those requests accept all drafts, so that owner receives 6 rows from every device of the group.
All inputs are finite; a program needn't handle non-finite values. Where the reference program divides by a largest or mean magnitude, that divisor is 1e-20 or more.
Results may differ from the reference program's by a relative error of at most 0.014.
Values may be sent and summed in bfloat16 or wider, within the bound.
No kernel may reach another device: no remote copies, remote signals or barrier semaphores. Data moves between devices by JAX's collectives and lax.ppermute only.
A program may use at most 256 MiB of HBM per device.

```python
import math
import jax
import jax.numpy as jnp
import numpy as np
from jax import lax

D = 7168
BLOCK = 128
FF_DEV = 256
TOP = 8
POS = 3
REQ_DEV = 8
FF = 1024
EXPERTS = 64
TOK_DEV = 24
TOKENS = 3072
CAP = 4
MCAP = 6
N_DP = 4
N_EXPERT = 32


def request_plan(key):
    devices = N_DP * N_EXPERT
    hub_key, perm_key, coin_key, take_key = jax.random.split(key, 4)
    hub = jax.random.randint(hub_key, (N_DP,), 0, N_EXPERT)
    orders = jax.vmap(lambda sub: jax.random.permutation(sub, N_EXPERT - 1))(jax.random.split(perm_key, devices))
    coin = jax.random.randint(coin_key, (devices, REQ_DEV), 0, 2)
    pair = jnp.arange(REQ_DEV, dtype=jnp.int32) // 2
    half = REQ_DEV // 2
    pick = jnp.where(coin == 1, pair[None, :] - 1, half + pair[None, :] - 2)
    pick = jnp.clip(pick, 0, N_EXPERT - 2)
    hub_device = jnp.repeat(hub, N_EXPERT)
    others = (hub_device[:, None] + 1 + jnp.take_along_axis(orders, pick, axis=1)) % N_EXPERT
    owner = jnp.where(pair[None, :] == 0, hub_device[:, None], others)
    taken = jax.random.randint(take_key, (devices, REQ_DEV), 0, POS)
    taken = jnp.where(pair[None, :] == 0, POS - 1, taken)
    return (owner.reshape(-1).astype(jnp.int32), taken.reshape(-1).astype(jnp.int32))


def draw_owner_map(key, part):
    owner, taken = request_plan(key)
    return owner


def draw_accepted(key, part):
    owner, taken = request_plan(key)
    return taken


def block_levels(own_key, shape, cuts, low, largest):
    loudness = 1.0
    for dim, blocks in cuts:
        heights = jax.random.uniform(jax.random.fold_in(jax.random.fold_in(own_key, 6), dim), (blocks,), jnp.float32, low / len(cuts), largest / len(cuts))
        loudness = loudness * jnp.repeat(jnp.exp(heights), shape[dim] // blocks).reshape((-1,) + (1,) * (len(shape) - 1 - dim))
    return loudness


def shared_out(own_key, own, number, rows, number_of, top, limit, skew):
    ranking = jax.random.permutation(own_key, number_of)
    crowded, common = load_shares(number_of, rows * top, limit, skew, True), load_shares(number_of, rows * top, limit, skew, False)
    places = jnp.arange(number_of)

    def named(tallies, turn):
        used = int((tallies > 0).sum())
        fixed = max(1, used // 4)
        moved = fixed + (places - fixed + turn * (used - fixed)) % max(1, number_of - fixed)
        return jnp.zeros((number_of,), jnp.int32).at[ranking[jnp.where(places < fixed, places, moved)]].set(jnp.asarray(tallies, jnp.int32))

    tallies = jnp.where(number % 4 == 0, named(crowded, number // 4), named(common, number - number // 4 - 1))
    mixed = jax.random.permutation(jax.random.fold_in(own, 3), number_of)
    donor, taker = mixed[0:number_of // 2 * 2:2], mixed[1:number_of // 2 * 2:2]
    margin = jnp.minimum(tallies[donor] - 1, limit - tallies[taker]) // 2
    margin = jnp.where((donor == ranking[0]) | (taker == ranking[0]) | (tallies[taker] == 0), 0, jnp.maximum(margin, 0))
    moved = jax.random.randint(jax.random.fold_in(own, 4), (number_of // 2,), 0, 1 << 20) % (margin + 1)
    tallies = tallies.at[donor].add(-moved).at[taker].add(moved)
    members = jnp.searchsorted(jnp.cumsum(tallies), jnp.arange(rows * top), side="right").astype(jnp.int32)
    grid = members.reshape(top, rows).T
    grid = grid[jax.random.permutation(jax.random.fold_in(own, 1), rows)]
    turn = jax.random.randint(jax.random.fold_in(own, 2), (rows, 1), 0, top)
    return jnp.take_along_axis(grid, (jnp.arange(top)[None, :] + turn) % top, axis=1)


def load_shares(amount, total, reach, skew, full):
    weights = [(1 << 20) // math.isqrt(rank ** skew) + 1 for rank in range(1, amount + 1)]
    largest = reach if full else min(reach, max(-(-total // amount), total * weights[0] // sum(weights)))
    least = 1 if total - largest >= amount - 1 else 0
    holding, rest = [largest] + [least] * (amount - 1), total - largest - least * (amount - 1)
    while rest > 0:
        free = [i for i in range(1, amount) if holding[i] < largest] or [i for i in range(1, amount) if holding[i] < reach]
        pool, left = sum([weights[i] for i in free]), rest
        for i in free:
            extra = min(reach - holding[i], max(1, left * weights[i] // pool), rest)
            holding[i] = holding[i] + extra
            rest = rest - extra
    return np.array(holding)


def noise(rng, dims, deviation, bound, cuts=(), kind=jnp.bfloat16):
    level = block_levels(rng, dims, cuts, -0.22, 0.18) if cuts else 1.0
    drawn = jax.random.normal(rng, dims, jnp.float32) * deviation * level
    return jnp.minimum(jnp.maximum(drawn, -bound), bound).astype(kind)


def setup_inputs(seed: int = 0) -> dict:
    seeds = jax.random.split(jax.random.key(seed), 10)
    hidden_rows = noise(seeds[0], (TOKENS, D), 1.0, 6.0, ((0, 128),))
    expert_ids_keys = jax.random.split(jax.random.fold_in(seeds[1], 1), TOKENS // TOK_DEV)
    expert_ids_turns = jax.random.permutation(jax.random.fold_in(seeds[1], 3), TOKENS // TOK_DEV)
    expert_ids = jax.vmap(lambda own, number: shared_out(jax.random.fold_in(seeds[1], 2), own, number, TOK_DEV, EXPERTS, TOP, CAP, 1))(expert_ids_keys, expert_ids_turns).reshape((TOKENS, TOP))
    gate_weights = jnp.clip(jnp.exp(math.log(0.5) - 2.3025851 * jax.random.uniform(seeds[2], (TOKENS, TOP), jnp.float32) ** block_levels(seeds[2], (TOKENS, TOP), ((0, 128),), -0.2, 0.2)), 0.05, 0.5)
    gate_matrix = noise(seeds[3], (EXPERTS, D, FF), D ** -0.5, 0.0625, ((0, 32), (2, 4)))
    up_matrix = noise(seeds[4], (EXPERTS, D, FF), D ** -0.5, 0.0625, ((0, 32), (2, 4)))
    down_matrix = noise(seeds[5], (EXPERTS, FF, D), FF ** -0.5, 0.1875, ((0, 32), (1, 4)))
    module_gain = jnp.clip(1.0 + 0.1 * jax.random.normal(seeds[6], (D,), jnp.float32), 0.5, 1.5)
    accepted = draw_accepted(jax.random.fold_in(seeds[9], 71), 0)
    owner_map = draw_owner_map(jax.random.fold_in(seeds[9], 71), 0)
    return {"hidden_rows": hidden_rows, "expert_ids": expert_ids, "gate_weights": gate_weights, "gate_matrix": gate_matrix, "up_matrix": up_matrix, "down_matrix": down_matrix, "module_gain": module_gain, "accepted": accepted, "owner_map": owner_map}


def quantize(rows):
    count, width = rows.shape
    blocks = rows.astype(jnp.float32).reshape(count, width // BLOCK, BLOCK)
    scales = lax.optimization_barrier(jnp.max(jnp.abs(blocks), axis=2)) + 1e-06
    quant = (blocks / scales[:, :, None]).astype(jnp.bfloat16).reshape(count, width)
    return (quant, scales)

def restore(quant, scales):
    lead = quant.shape[:-1]
    nblocks = scales.shape[-1]
    blocks = quant.astype(jnp.float32).reshape(lead + (nblocks, quant.shape[-1] // nblocks))
    return (blocks * scales[..., None]).reshape(quant.shape).astype(jnp.bfloat16)

def assign_slots(ids, experts):
    flat = ids.reshape(-1)
    onehot = (flat[:, None] == jnp.arange(experts, dtype=jnp.int32)[None, :]).astype(jnp.int32)
    before = jnp.cumsum(onehot, axis=0) - onehot
    return (flat, lax.optimization_barrier(jnp.sum(before * onehot, axis=1)).astype(jnp.int32))

def normalize(rows, gain):
    values = rows.astype(jnp.float32)
    factor = lax.rsqrt(lax.optimization_barrier(jnp.mean(values * values, axis=-1, keepdims=True)) + 1e-06)
    return (values * factor * gain).astype(jnp.bfloat16)

def pack_module(normed, accepted, owner_map, owners):
    count = normed.shape[0]
    requests = accepted.shape[0]
    per_request = count // requests
    capacity = 2 * per_request
    position = jnp.arange(count, dtype=jnp.int32)
    request = position // per_request
    place = position % per_request
    sizes = accepted + 1
    same = owner_map[:, None] == owner_map[None, :]
    earlier = jnp.arange(requests, dtype=jnp.int32)[:, None] > jnp.arange(requests, dtype=jnp.int32)[None, :]
    start = lax.optimization_barrier(jnp.sum(jnp.where(same & earlier, sizes[None, :], 0), axis=1)).astype(jnp.int32)
    live = place <= accepted[request]
    target = owner_map[request] * capacity + start[request] + place
    choose = (target[None, :] == jnp.arange(owners * capacity, dtype=jnp.int32)[:, None]) & live[None, :]
    packed = jnp.dot(choose.astype(jnp.bfloat16), normed, preferred_element_type=jnp.float32).astype(jnp.bfloat16)
    return packed.reshape(owners, capacity, normed.shape[1])

def reference(hidden_rows, expert_ids, gate_weights, gate_matrix, up_matrix, down_matrix, module_gain, accepted, owner_map):
    devices = N_DP * N_EXPERT
    quant, scales = quantize(hidden_rows)
    restored = restore(quant, scales)
    padded = jnp.concatenate([restored, jnp.zeros((1, D), jnp.bfloat16)], axis=0)
    flat_ids = expert_ids.reshape(devices, TOK_DEV * TOP)

    def device_slots(ids):
        return assign_slots(ids, EXPERTS)[1]
    slots = jax.vmap(device_slots)(flat_ids)
    device_index = jnp.broadcast_to(jnp.arange(devices, dtype=jnp.int32)[:, None], flat_ids.shape)
    token_index = device_index * TOK_DEV + (jnp.arange(TOK_DEV * TOP, dtype=jnp.int32) // TOP)[None, :]
    table = jnp.full((EXPERTS, devices, CAP), TOKENS, jnp.int32).at[flat_ids, device_index, slots].set(token_index)
    weight_table = jnp.zeros((EXPERTS, devices, CAP), jnp.float32).at[flat_ids, device_index, slots].set(gate_weights.reshape(devices, TOK_DEV * TOP))

    def one_expert(total, inputs):
        rows_index, weights, gate_one, up_one, down_one = inputs
        index = rows_index.reshape(-1)
        rows = padded[index]
        gate = jnp.dot(rows, gate_one, preferred_element_type=jnp.float32)
        up = jnp.dot(rows, up_one, preferred_element_type=jnp.float32)
        act = (jax.nn.silu(gate) * up).astype(jnp.bfloat16)
        quarters = jnp.einsum('rqf,qfd->rqd', act.astype(jnp.float32).reshape(-1, N_DP, FF_DEV), down_one.astype(jnp.float32).reshape(N_DP, FF_DEV, D), precision=lax.Precision.HIGHEST).astype(jnp.bfloat16)
        output = lax.optimization_barrier(jnp.sum(quarters.astype(jnp.float32), axis=1))
        total = total.at[index].add(weights.reshape(-1)[:, None] * output)
        return (total, None)
    total, _ = lax.scan(one_expert, jnp.zeros((TOKENS + 1, D), jnp.float32), (table, weight_table, gate_matrix, up_matrix, down_matrix))
    final_rows = (hidden_rows.astype(jnp.float32) + total[:TOKENS]).astype(jnp.bfloat16)
    normed = normalize(final_rows, module_gain)

    def device_pack(rows, taken, owners_of):
        return pack_module(rows, taken, owners_of, N_EXPERT)
    packed = jax.vmap(device_pack)(normed.reshape(devices, TOK_DEV, D), accepted.reshape(devices, REQ_DEV), owner_map.reshape(devices, REQ_DEV))
    module_rows = jnp.transpose(packed.reshape(N_DP, N_EXPERT, N_EXPERT, MCAP, D), (0, 2, 1, 3, 4))
    return (final_rows, module_rows)
```

```python
import jax
import jax.numpy as jnp
from jax import lax
from jax.sharding import PartitionSpec as P

AXES = ("dp", "expert")
RING = 4
CORES = 2
STRIDE = {"y": 32, "x": 8, "z": 2}
ORDERS = (("z", "y", "x"), ("x", "z", "y"), ("y", "x", "z"))
META = 128


def swap(value, axis, link):
    stride = STRIDE[axis]
    pairs = []
    for device in range(RING ** 3 * CORES):
        place = device // stride % RING
        flip = 1 if device % CORES == link else 3
        pairs.append((device, device + ((place ^ flip) - place) * stride))
    return lax.ppermute(value, AXES, pairs)


def from_sibling(value):
    devices = RING ** 3 * CORES
    return lax.ppermute(value, AXES, [(device, device ^ 1) for device in range(devices)])


def spread_weights(ids, weights, experts):
    hits = ids[:, :, None] == jnp.arange(experts, dtype=jnp.int32)[None, None, :]
    table = jnp.sum(jnp.where(hits, weights[:, :, None], 0.0), axis=1)
    high = table.astype(jnp.bfloat16)
    low = (table - high.astype(jnp.float32)).astype(jnp.bfloat16)
    return jnp.concatenate([high, low], axis=1)


def normalize(rows, gain):
    values = rows.astype(jnp.float32)
    factor = lax.rsqrt(jnp.mean(values * values, axis=-1, keepdims=True) + 1e-06)
    return (values * factor * gain).astype(jnp.bfloat16)


def pack_module(normed, accepted, owner_map, owners):
    count = normed.shape[0]
    requests = accepted.shape[0]
    per_request = count // requests
    capacity = 2 * per_request
    position = jnp.arange(count, dtype=jnp.int32)
    request = position // per_request
    place = position % per_request
    sizes = accepted + 1
    same = owner_map[:, None] == owner_map[None, :]
    earlier = (
        jnp.arange(requests, dtype=jnp.int32)[:, None]
        > jnp.arange(requests, dtype=jnp.int32)[None, :]
    )
    start = jnp.sum(jnp.where(same & earlier, sizes[None, :], 0), axis=1)
    live = place <= accepted[request]
    target = owner_map[request] * capacity + start[request] + place
    choose = (target[None, :] == jnp.arange(owners * capacity, dtype=jnp.int32)[:, None]) & live[
        None, :
    ]
    packed = jnp.dot(
        choose.astype(jnp.bfloat16), normed, preferred_element_type=jnp.float32
    ).astype(jnp.bfloat16)
    return packed.reshape(owners, capacity, normed.shape[1])


def body(
    hidden_rows,
    expert_ids,
    gate_weights,
    gate_matrix,
    up_matrix,
    down_matrix,
    module_gain,
    accepted,
    owner_map,
):
    owners = lax.axis_size("expert")
    local, width, hidden = gate_matrix.shape
    experts = local * owners
    count = hidden_rows.shape[0]
    parts = len(ORDERS)
    part = count // parts

    meta = spread_weights(expert_ids, gate_weights, experts)
    wide = jnp.concatenate([hidden_rows, meta], axis=1)

    gates = (gate_matrix, from_sibling(gate_matrix))
    ups = (up_matrix, from_sibling(up_matrix))
    downs = (down_matrix, from_sibling(down_matrix))
    enter = jnp.concatenate(
        [pair[e] for both in (gates, ups) for pair in both for e in range(local)], axis=1
    )
    enter = jnp.concatenate([enter, jnp.zeros((META, enter.shape[1]), enter.dtype)], axis=0)
    leave = jnp.concatenate([d.reshape(local * hidden, width) for d in downs], axis=0)
    mine = lax.axis_index("expert")
    column = jnp.arange(2 * local * hidden, dtype=jnp.int32) // hidden
    named = jnp.where(column < local, mine * local + column, (mine ^ 1) * local + column - local)
    expand = (
        jnp.arange(META, dtype=jnp.int32)[:, None] % experts == named[None, :]
    ).astype(jnp.bfloat16)

    blocks = [wide[p * part : (p + 1) * part] for p in range(parts)]
    for phase in (0, 1):
        for link in (0, 1):
            got = [swap(block, order[phase], link) for block, order in zip(blocks, ORDERS)]
            blocks = [jnp.concatenate(pair, axis=0) for pair in zip(blocks, got)]

    def outputs(pieces):
        rows = jnp.concatenate(pieces, axis=0)
        raised = jnp.dot(rows, enter, preferred_element_type=jnp.float32)
        share = jnp.dot(rows[:, width:], expand, preferred_element_type=jnp.float32)
        half = raised.shape[1] // 2
        act = (jax.nn.silu(raised[:, :half]) * raised[:, half:] * share).astype(jnp.bfloat16)
        result = jnp.dot(act, leave, preferred_element_type=jnp.float32).astype(jnp.bfloat16)
        size = pieces[0].shape[0]
        return [result[p * size : (p + 1) * size] for p in range(parts)]

    def swap_last(values, link):
        return [swap(value, order[2], link) for value, order in zip(values, ORDERS)]

    def add(*values):
        return sum(value.astype(jnp.float32) for value in values)

    near = swap_last(blocks, 0)
    next_ = swap_last(blocks, 1)
    across = swap_last(near, 1)
    out_near = outputs(near)
    out_next = outputs(next_)
    out_across = outputs(across)
    out_own = outputs(blocks)
    from_next = swap_last(out_next, 1)
    for_near = swap_last(out_across, 1)
    for_near = [add(a, b).astype(jnp.bfloat16) for a, b in zip(out_near, for_near)]
    from_near = swap_last(for_near, 0)
    totals = [add(*terms) for terms in zip(out_own, from_next, from_near)]
    for phase in (1, 0):
        for link in (1, 0):
            half = totals[0].shape[0] // 2
            got = [
                swap(total[half:].astype(jnp.bfloat16), order[phase], link)
                for total, order in zip(totals, ORDERS)
            ]
            totals = [add(total[:half], other) for total, other in zip(totals, got)]
    update = jnp.concatenate(totals, axis=0)

    final_rows = (hidden_rows.astype(jnp.float32) + update).astype(jnp.bfloat16)
    normed = normalize(final_rows, module_gain)
    packed = pack_module(normed, accepted, owner_map, owners)
    delivered = lax.all_to_all(packed, "expert", split_axis=0, concat_axis=0, tiled=True)
    return (final_rows, delivered[None, None])


def solution(mesh):
    return jax.shard_map(
        body,
        mesh=mesh,
        in_specs=(
            P(("dp", "expert"), None),
            P(("dp", "expert"), None),
            P(("dp", "expert"), None),
            P("expert", None, "dp"),
            P("expert", None, "dp"),
            P("expert", "dp", None),
            P(),
            P(("dp", "expert")),
            P(("dp", "expert")),
        ),
        out_specs=(P(("dp", "expert"), None), P("dp", "expert", None, None, None)),
        check_vma=False,
    )
```

```python
import functools

import jax
import jax.numpy as jnp
from jax import lax
from jax.experimental import pallas as pl
from jax.experimental.pallas import tpu as pltpu
from jax.sharding import PartitionSpec as P

AXES = ("dp", "expert")
RING = 4
CORES = 2
STRIDE = {"y": 32, "x": 8, "z": 2}
ORDERS = (("z", "y", "x"), ("x", "z", "y"), ("y", "x", "z"))
META = 128
ENTER_STEPS = 2
LEAVE_STEPS = 4
VMEM_LIMIT = 48 * 1024 * 1024


def swap(value, axis, link):
    stride = STRIDE[axis]
    pairs = []
    for device in range(RING ** 3 * CORES):
        place = device // stride % RING
        flip = 1 if device % CORES == link else 3
        pairs.append((device, device + ((place ^ flip) - place) * stride))
    return lax.ppermute(value, AXES, pairs)


def from_sibling(value):
    devices = RING ** 3 * CORES
    return lax.ppermute(value, AXES, [(device, device ^ 1) for device in range(devices)])


def enter_kernel(steps, *refs):
    parts = len(ORDERS)
    rows, metas = refs[:parts], refs[parts : 2 * parts]
    gates, ups = refs[2 * parts : 2 * parts + 2], refs[2 * parts + 2 : 2 * parts + 4]
    expand, act, held, gate_sum, up_sum = refs[2 * parts + 4 :]
    expert, step = pl.program_id(0), pl.program_id(1)
    size, depth = rows[0].shape
    local = pl.num_programs(0) // 2
    here = pl.ds(pl.multiple_of(step * depth, depth), depth)

    @pl.when(expert == 0)
    def _():
        for p in range(parts):
            held[p * size : (p + 1) * size, here] = rows[p][...]

    def multiply(gate, up):
        block = held[:, here]
        gate_part = jnp.dot(block, gate[0], preferred_element_type=jnp.float32)
        up_part = jnp.dot(block, up[0], preferred_element_type=jnp.float32)

        @pl.when(step == 0)
        def _():
            gate_sum[...] = gate_part
            up_sum[...] = up_part

        @pl.when(step > 0)
        def _():
            gate_sum[...] += gate_part
            up_sum[...] += up_part

    for which in range(2):
        pl.when(expert // local == which)(
            functools.partial(multiply, gates[which], ups[which])
        )

    @pl.when(step == steps - 1)
    def _():
        meta = jnp.concatenate([ref[...] for ref in metas], axis=0)
        share = jnp.dot(meta, expand[...], preferred_element_type=jnp.float32)
        gate = gate_sum[...]
        act[...] = (gate / (1.0 + jnp.exp(-gate)) * up_sum[...] * share).astype(act.dtype)


def enter(pieces, gates, ups, expand):
    size, wide = pieces[0].shape
    local, width, hidden = gates[0].shape
    parts, steps = len(pieces), ENTER_STEPS
    depth = width // steps
    count = parts * size
    last = steps - 1

    def weights(which):
        def index(expert, step):
            early, late = expert < which * local, expert >= (which + 1) * local
            place = jnp.where(early, 0, jnp.where(late, local - 1, expert - which * local))
            return place, jnp.where(early, 0, jnp.where(late, last, step)), 0

        return pl.BlockSpec((1, depth, hidden), index)

    return pl.pallas_call(
        functools.partial(enter_kernel, steps),
        grid=(2 * local, steps),
        out_shape=jax.ShapeDtypeStruct((count, 2 * local * hidden), jnp.bfloat16),
        in_specs=[
            pl.BlockSpec((size, depth), lambda e, k: (0, jnp.where(e == 0, k, last)))
        ] * parts
        + [pl.BlockSpec((size, META), lambda e, k: (0, width // META))] * parts
        + [weights(0), weights(1)] * 2
        + [pl.BlockSpec((META, hidden), lambda e, k: (0, e))],
        out_specs=pl.BlockSpec((count, hidden), lambda e, k: (0, e)),
        scratch_shapes=[
            pltpu.VMEM((count, width), jnp.bfloat16),
            pltpu.VMEM((count, hidden), jnp.float32),
            pltpu.VMEM((count, hidden), jnp.float32),
        ],
        compiler_params=pltpu.CompilerParams(vmem_limit_bytes=VMEM_LIMIT),
        cost_estimate=pl.CostEstimate(
            flops=8 * count * width * local * hidden,
            bytes_accessed=8 * local * width * hidden + 2 * count * wide,
            transcendentals=2 * count * local * hidden,
        ),
        name="enter",
    )(*pieces, *pieces, *gates, *ups, expand)


def leave_kernel(act, own, other, *outs):
    half = own.shape[0]
    result = jnp.dot(act[:, :half], own[...], preferred_element_type=jnp.float32)
    result += jnp.dot(act[:, half:], other[...], preferred_element_type=jnp.float32)
    size = outs[0].shape[0]
    for p, out in enumerate(outs):
        out[...] = result[p * size : (p + 1) * size].astype(out.dtype)


def leave(act, downs, parts):
    count, inner = act.shape
    half, width = downs[0].shape
    tile, size = width // LEAVE_STEPS, count // parts
    return pl.pallas_call(
        leave_kernel,
        grid=(LEAVE_STEPS,),
        out_shape=[jax.ShapeDtypeStruct((size, width), jnp.bfloat16)] * parts,
        in_specs=[pl.BlockSpec((count, inner), lambda n: (0, 0))]
        + [pl.BlockSpec((half, tile), lambda n: (0, n))] * 2,
        out_specs=[pl.BlockSpec((size, tile), lambda n: (0, n))] * parts,
        compiler_params=pltpu.CompilerParams(vmem_limit_bytes=VMEM_LIMIT),
        cost_estimate=pl.CostEstimate(
            flops=2 * count * inner * width,
            bytes_accessed=2 * (inner * width + count * width + count * inner),
            transcendentals=0,
        ),
        name="leave",
    )(act, *downs)


def together(*values):
    return lax.optimization_barrier(values)


def spread_weights(ids, weights, experts):
    hits = ids[:, :, None] == jnp.arange(experts, dtype=jnp.int32)[None, None, :]
    table = jnp.sum(jnp.where(hits, weights[:, :, None], 0.0), axis=1)
    high = table.astype(jnp.bfloat16)
    low = (table - high.astype(jnp.float32)).astype(jnp.bfloat16)
    return jnp.concatenate([high, low], axis=1)


def normalize(rows, gain):
    values = rows.astype(jnp.float32)
    factor = lax.rsqrt(jnp.mean(values * values, axis=-1, keepdims=True) + 1e-06)
    return (values * factor * gain).astype(jnp.bfloat16)


def pack_module(normed, accepted, owner_map, owners):
    count = normed.shape[0]
    requests = accepted.shape[0]
    per_request = count // requests
    capacity = 2 * per_request
    position = jnp.arange(count, dtype=jnp.int32)
    request = position // per_request
    place = position % per_request
    sizes = accepted + 1
    same = owner_map[:, None] == owner_map[None, :]
    earlier = (
        jnp.arange(requests, dtype=jnp.int32)[:, None]
        > jnp.arange(requests, dtype=jnp.int32)[None, :]
    )
    start = jnp.sum(jnp.where(same & earlier, sizes[None, :], 0), axis=1)
    live = place <= accepted[request]
    target = owner_map[request] * capacity + start[request] + place
    choose = (target[None, :] == jnp.arange(owners * capacity, dtype=jnp.int32)[:, None]) & live[
        None, :
    ]
    packed = jnp.dot(
        choose.astype(jnp.bfloat16), normed, preferred_element_type=jnp.float32
    ).astype(jnp.bfloat16)
    return packed.reshape(owners, capacity, normed.shape[1])


def body(
    hidden_rows,
    expert_ids,
    gate_weights,
    gate_matrix,
    up_matrix,
    down_matrix,
    module_gain,
    accepted,
    owner_map,
):
    owners = lax.axis_size("expert")
    local, width, hidden = gate_matrix.shape
    experts = local * owners
    count = hidden_rows.shape[0]
    parts = len(ORDERS)
    part = count // parts

    meta = spread_weights(expert_ids, gate_weights, experts)
    wide = jnp.concatenate([hidden_rows, meta], axis=1)

    gates = (gate_matrix, from_sibling(gate_matrix))
    ups = (up_matrix, from_sibling(up_matrix))
    down_rows = down_matrix.reshape(local * hidden, width)
    downs = (down_rows, from_sibling(down_rows))
    mine = lax.axis_index("expert")
    column = jnp.arange(2 * local * hidden, dtype=jnp.int32) // hidden
    named = jnp.where(column < local, mine * local + column, (mine ^ 1) * local + column - local)
    expand = (
        jnp.arange(META, dtype=jnp.int32)[:, None] % experts == named[None, :]
    ).astype(jnp.bfloat16)

    blocks = [wide[p * part : (p + 1) * part] for p in range(parts)]
    for phase in (0, 1):
        for link in (0, 1):
            got = [swap(block, order[phase], link) for block, order in zip(blocks, ORDERS)]
            blocks, got = together(blocks, got)
            blocks = [jnp.concatenate(pair, axis=0) for pair in zip(blocks, got)]

    def outputs(pieces):
        return leave(enter(pieces, gates, ups, expand), downs, parts)

    def swap_last(values, link):
        return [swap(value, order[2], link) for value, order in zip(values, ORDERS)]

    def add(*values):
        return sum(value.astype(jnp.float32) for value in values)

    near = swap_last(blocks, 0)
    blocks, near = together(blocks, near)
    following = swap_last(blocks, 1)
    near, following = together(near, following)
    across = swap_last(near, 1)
    out_following = outputs(following)
    out_following, across = together(out_following, across)
    from_following = swap_last(out_following, 1)
    out_across = outputs(across)
    out_across, from_following, near = together(out_across, from_following, near)
    for_near = swap_last(out_across, 1)
    out_near = outputs(near)
    for_near, out_near, blocks = together(for_near, out_near, blocks)
    for_near = [add(a, b).astype(jnp.bfloat16) for a, b in zip(out_near, for_near)]
    from_near = swap_last(for_near, 0)
    out_own = outputs(blocks)
    from_near, out_own = together(from_near, out_own)
    terms = list(zip(out_own, from_following, from_near))
    for phase in (1, 0):
        for link in (1, 0):
            half = terms[0][0].shape[0] // 2
            sent = [add(*[t[half:] for t in ts]).astype(jnp.bfloat16) for ts in terms]
            got = [swap(value, order[phase], link) for value, order in zip(sent, ORDERS)]
            kept = [add(*[t[:half] for t in ts]) for ts in terms]
            kept, got = together(kept, got)
            terms = list(zip(kept, got))
    update = jnp.concatenate([add(*ts) for ts in terms], axis=0)

    final_rows = (hidden_rows.astype(jnp.float32) + update).astype(jnp.bfloat16)
    normed = normalize(final_rows, module_gain)
    packed = pack_module(normed, accepted, owner_map, owners)
    delivered = lax.all_to_all(packed, "expert", split_axis=0, concat_axis=0, tiled=True)
    return (final_rows, delivered[None, None])


def solution(mesh):
    return jax.shard_map(
        body,
        mesh=mesh,
        in_specs=(
            P(("dp", "expert"), None),
            P(("dp", "expert"), None),
            P(("dp", "expert"), None),
            P("expert", None, "dp"),
            P("expert", None, "dp"),
            P("expert", "dp", None),
            P(),
            P(("dp", "expert")),
            P(("dp", "expert")),
        ),
        out_specs=(P(("dp", "expert"), None), P("dp", "expert", None, None, None)),
        check_vma=False,
    )
```

```python
import functools

import jax
import jax.numpy as jnp
from jax import lax
from jax.experimental import pallas as pl
from jax.experimental.pallas import tpu as pltpu
from jax.sharding import PartitionSpec as P

AXES = ("dp", "expert")
RING = 4
CORES = 2
STRIDE = {"y": 32, "x": 8, "z": 2}
ORDERS = (("z", "y", "x"), ("x", "z", "y"), ("y", "x", "z"))
META = 128
DEPTH = 3584
TILE = 1792
SLOTS = 3
VMEM_LIMIT = 40 * 1024 * 1024


def swap(value, axis, link):
    stride = STRIDE[axis]
    pairs = []
    for device in range(RING ** 3 * CORES):
        place = device // stride % RING
        flip = 1 if device % CORES == link else 3
        pairs.append((device, device + ((place ^ flip) - place) * stride))
    return lax.ppermute(value, AXES, pairs)


def from_sibling(value):
    devices = RING ** 3 * CORES
    return lax.ppermute(value, AXES, [(device, device ^ 1) for device in range(devices)])


def experts_kernel(local, *refs):
    parts = len(ORDERS)
    rows, refs = refs[:parts], refs[parts:]
    gates, ups, downs, expand, refs = refs[0:2], refs[2:4], refs[4:6], refs[6], refs[7:]
    outs, refs = refs[:parts], refs[parts:]
    held, raised, sums, act, lowered, done = refs[:6]
    row_sem, meta_sem, raise_sem, lower_sem, out_sem = refs[6:]
    size, width = rows[0].shape[0], rows[0].shape[1] - META
    hidden = sums.shape[1] // 2
    steps, tiles = width // DEPTH, width // TILE
    total = 2 * local * steps
    half = downs[0].shape[0]
    ahead = SLOTS - 1

    def row_copy(p, step):
        here = pl.ds(pl.multiple_of(step * DEPTH, DEPTH), DEPTH)
        return pltpu.make_async_copy(
            rows[p].at[:, here], held.at[pl.ds(p * size, size), here], row_sem.at[p, step]
        )

    def meta_copy(p):
        here = pl.ds(width, META)
        return pltpu.make_async_copy(
            rows[p].at[:, here], held.at[pl.ds(p * size, size), here], meta_sem.at[p]
        )

    def raise_copies(which, turn):
        slot, step = turn % SLOTS, turn % steps
        expert = turn // steps % local
        here = pl.ds(pl.multiple_of(step * DEPTH, DEPTH), DEPTH)
        return [
            pltpu.make_async_copy(
                source[which].at[expert, here, :],
                raised.at[slot, :, pl.ds(n * hidden, hidden)],
                raise_sem.at[slot, n],
            )
            for n, source in enumerate((gates, ups))
        ]

    def lower_copies(tile):
        slot = tile % SLOTS
        here = pl.ds(pl.multiple_of(tile * TILE, TILE), TILE)
        return [
            pltpu.make_async_copy(
                downs[n].at[:, here],
                lowered.at[slot, pl.ds(n * half, half), :],
                lower_sem.at[slot, n],
            )
            for n in range(2)
        ]

    def out_copies(tile):
        slot = tile % 2
        here = pl.ds(pl.multiple_of(tile * TILE, TILE), TILE)
        return [
            pltpu.make_async_copy(
                done.at[slot, pl.ds(p * size, size), :], outs[p].at[:, here], out_sem.at[slot, p]
            )
            for p in range(parts)
        ]

    def start_raise(turn):
        for which in range(2):

            @pl.when(turn // (steps * local) == which)
            def _():
                for copy in raise_copies(which, turn):
                    copy.start()

    def start_lower(tile):
        for copy in lower_copies(tile):
            copy.start()

    for p in range(parts):
        row_copy(p, 0).start()
    for copy in raise_copies(0, 0):
        copy.start()
    for p in range(parts):
        meta_copy(p).start()
    for turn in range(1, ahead):
        for copy in raise_copies(0, turn):
            copy.start()
        for p in range(parts):
            row_copy(p, turn).start()
    for step in range(ahead, steps):
        for p in range(parts):
            row_copy(p, step).start()

    @pl.loop(0, total)
    def _(turn):
        step, expert = turn % steps, turn // steps
        later = turn + ahead

        @pl.when(later < total)
        def _():
            start_raise(later)

        @pl.when(later >= total)
        def _():
            start_lower(later - total)

        @pl.when(turn < steps)
        def _():
            for p in range(parts):
                row_copy(p, step).wait()

        @pl.when(turn == 0)
        def _():
            for p in range(parts):
                meta_copy(p).wait()

        for copy in raise_copies(0, turn):
            copy.wait()
        slot = turn % SLOTS
        block = held[:, pl.ds(pl.multiple_of(step * DEPTH, DEPTH), DEPTH)]
        both = jnp.dot(block, raised[slot], preferred_element_type=jnp.float32)

        @pl.when(step == 0)
        def _():
            sums[...] = both

        @pl.when(step > 0)
        def _():
            sums[...] += both

        @pl.when(step == steps - 1)
        def _():
            mine = pl.ds(pl.multiple_of(expert * hidden, hidden), hidden)
            share = jnp.dot(
                held[:, width:], expand[:, mine], preferred_element_type=jnp.float32
            )
            gate, up = sums[:, :hidden], sums[:, hidden:]
            act[:, mine] = (gate / (1.0 + jnp.exp(-gate)) * up * share).astype(act.dtype)

    @pl.loop(0, tiles)
    def _(tile):
        @pl.when(tile + ahead < tiles)
        def _():
            start_lower(tile + ahead)

        for copy in lower_copies(tile):
            copy.wait()

        @pl.when(tile >= 2)
        def _():
            for copy in out_copies(tile - 2):
                copy.wait()

        result = jnp.dot(act[...], lowered[tile % SLOTS], preferred_element_type=jnp.float32)
        done[tile % 2] = result.astype(done.dtype)
        for copy in out_copies(tile):
            copy.start()

    for tile in range(tiles - 2, tiles):
        for copy in out_copies(tile):
            copy.wait()


def experts_of(pieces, gates, ups, downs, expand):
    size, wide = pieces[0].shape
    local, width, hidden = gates[0].shape
    parts = len(pieces)
    count, inner = parts * size, 2 * local * hidden
    anywhere = pl.BlockSpec(memory_space=pl.ANY)
    return pl.pallas_call(
        functools.partial(experts_kernel, local),
        out_shape=[jax.ShapeDtypeStruct((size, width), jnp.bfloat16)] * parts,
        in_specs=[anywhere] * (parts + 6) + [pl.BlockSpec(memory_space=pltpu.VMEM)],
        out_specs=[anywhere] * parts,
        scratch_shapes=[
            pltpu.VMEM((count, wide), jnp.bfloat16),
            pltpu.VMEM((SLOTS, DEPTH, 2 * hidden), jnp.bfloat16),
            pltpu.VMEM((count, 2 * hidden), jnp.float32),
            pltpu.VMEM((count, inner), jnp.bfloat16),
            pltpu.VMEM((SLOTS, inner, TILE), jnp.bfloat16),
            pltpu.VMEM((2, count, TILE), jnp.bfloat16),
            pltpu.SemaphoreType.DMA((parts, width // DEPTH)),
            pltpu.SemaphoreType.DMA((parts,)),
            pltpu.SemaphoreType.DMA((SLOTS, 2)),
            pltpu.SemaphoreType.DMA((SLOTS, 2)),
            pltpu.SemaphoreType.DMA((2, parts)),
        ],
        compiler_params=pltpu.CompilerParams(vmem_limit_bytes=VMEM_LIMIT),
        cost_estimate=pl.CostEstimate(
            flops=6 * count * width * inner,
            bytes_accessed=6 * width * inner + 4 * count * wide,
            transcendentals=count * inner,
        ),
        name="experts",
    )(*pieces, *gates, *ups, *downs, expand)


def together(*values):
    return lax.optimization_barrier(values)


def spread_weights(ids, weights, experts):
    hits = ids[:, :, None] == jnp.arange(experts, dtype=jnp.int32)[None, None, :]
    table = jnp.sum(jnp.where(hits, weights[:, :, None], 0.0), axis=1)
    high = table.astype(jnp.bfloat16)
    low = (table - high.astype(jnp.float32)).astype(jnp.bfloat16)
    return jnp.concatenate([high, low], axis=1)


def normalize(rows, gain):
    values = rows.astype(jnp.float32)
    factor = lax.rsqrt(jnp.mean(values * values, axis=-1, keepdims=True) + 1e-06)
    return (values * factor * gain).astype(jnp.bfloat16)


def pack_module(normed, accepted, owner_map, owners):
    count = normed.shape[0]
    requests = accepted.shape[0]
    per_request = count // requests
    capacity = 2 * per_request
    position = jnp.arange(count, dtype=jnp.int32)
    request = position // per_request
    place = position % per_request
    sizes = accepted + 1
    same = owner_map[:, None] == owner_map[None, :]
    earlier = (
        jnp.arange(requests, dtype=jnp.int32)[:, None]
        > jnp.arange(requests, dtype=jnp.int32)[None, :]
    )
    start = jnp.sum(jnp.where(same & earlier, sizes[None, :], 0), axis=1)
    live = place <= accepted[request]
    target = owner_map[request] * capacity + start[request] + place
    choose = (target[None, :] == jnp.arange(owners * capacity, dtype=jnp.int32)[:, None]) & live[
        None, :
    ]
    packed = jnp.dot(
        choose.astype(jnp.bfloat16), normed, preferred_element_type=jnp.float32
    ).astype(jnp.bfloat16)
    return packed.reshape(owners, capacity, normed.shape[1])


def body(
    hidden_rows,
    expert_ids,
    gate_weights,
    gate_matrix,
    up_matrix,
    down_matrix,
    module_gain,
    accepted,
    owner_map,
):
    owners = lax.axis_size("expert")
    local, width, hidden = gate_matrix.shape
    experts = local * owners
    count = hidden_rows.shape[0]
    parts = len(ORDERS)
    part = count // parts

    meta = spread_weights(expert_ids, gate_weights, experts)
    wide = jnp.concatenate([hidden_rows, meta], axis=1)

    mine = lax.axis_index("expert")
    column = jnp.arange(2 * local * hidden, dtype=jnp.int32) // hidden
    named = jnp.where(column < local, mine * local + column, (mine ^ 1) * local + column - local)
    expand = (
        jnp.arange(META, dtype=jnp.int32)[:, None] % experts == named[None, :]
    ).astype(jnp.bfloat16)

    weights = [gate_matrix, up_matrix, down_matrix.reshape(local * hidden, width)]
    others = []
    blocks = [wide[p * part : (p + 1) * part] for p in range(parts)]
    for phase in (0, 1):
        for link in (0, 1):
            got = [swap(block, order[phase], link) for block, order in zip(blocks, ORDERS)]
            if len(others) < len(weights):
                others.append(from_sibling(weights[len(others)]))
            blocks, got, others = together(blocks, got, others)
            blocks = [jnp.concatenate(pair, axis=0) for pair in zip(blocks, got)]
    gates, ups, downs = zip(weights, others)

    def outputs(pieces):
        return experts_of(pieces, gates, ups, downs, expand)

    def swap_last(values, link):
        return [swap(value, order[2], link) for value, order in zip(values, ORDERS)]

    def add(*values):
        return sum(value.astype(jnp.float32) for value in values)

    near = swap_last(blocks, 0)
    out_own = outputs(blocks)
    near, blocks, out_own = together(near, blocks, out_own)
    following = swap_last(blocks, 1)
    out_near = outputs(near)
    following, near, out_near = together(following, near, out_near)
    across = swap_last(near, 1)
    out_following = outputs(following)
    across, out_following = together(across, out_following)
    from_following = swap_last(out_following, 1)
    out_across = outputs(across)
    from_following, out_across = together(from_following, out_across)
    for_near = swap_last(out_across, 1)
    for_near = [add(a, b).astype(jnp.bfloat16) for a, b in zip(out_near, for_near)]
    from_near = swap_last(for_near, 0)
    terms = list(zip(out_own, from_following, from_near))
    for phase in (1, 0):
        for link in (1, 0):
            half = terms[0][0].shape[0] // 2
            sent = [add(*[t[half:] for t in ts]).astype(jnp.bfloat16) for ts in terms]
            got = [swap(value, order[phase], link) for value, order in zip(sent, ORDERS)]
            kept = [add(*[t[:half] for t in ts]) for ts in terms]
            kept, got = together(kept, got)
            terms = list(zip(kept, got))
    update = jnp.concatenate([add(*ts) for ts in terms], axis=0)

    final_rows = (hidden_rows.astype(jnp.float32) + update).astype(jnp.bfloat16)
    normed = normalize(final_rows, module_gain)
    packed = pack_module(normed, accepted, owner_map, owners)
    delivered = lax.all_to_all(packed, "expert", split_axis=0, concat_axis=0, tiled=True)
    return (final_rows, delivered[None, None])


def solution(mesh):
    return jax.shard_map(
        body,
        mesh=mesh,
        in_specs=(
            P(("dp", "expert"), None),
            P(("dp", "expert"), None),
            P(("dp", "expert"), None),
            P("expert", None, "dp"),
            P("expert", None, "dp"),
            P("expert", "dp", None),
            P(),
            P(("dp", "expert")),
            P(("dp", "expert")),
        ),
        out_specs=(P(("dp", "expert"), None), P("dp", "expert", None, None, None)),
        check_vma=False,
    )
```

```python
import functools

import jax
import jax.numpy as jnp
from jax import lax
from jax.experimental import pallas as pl
from jax.experimental.pallas import tpu as pltpu
from jax.sharding import PartitionSpec as P

AXES = ("dp", "expert")
RING = 4
CORES = 2
STRIDE = {"y": 32, "x": 8, "z": 2}
ORDERS = (("z", "y", "x"), ("x", "z", "y"), ("y", "x", "z"))
META = 128
LANES = 128
DEPTH = 3584
TILE = 1792
SLOTS = 3
VMEM_LIMIT = 40 * 1024 * 1024


def swap(value, axis, link):
    stride = STRIDE[axis]
    pairs = []
    for device in range(RING ** 3 * CORES):
        place = device // stride % RING
        flip = 1 if device % CORES == link else 3
        pairs.append((device, device + ((place ^ flip) - place) * stride))
    return lax.ppermute(value, AXES, pairs)


def from_sibling(value):
    devices = RING ** 3 * CORES
    return lax.ppermute(value, AXES, [(device, device ^ 1) for device in range(devices)])


def experts_kernel(local, added, *refs):
    parts = len(ORDERS)
    rows, refs = refs[:parts], refs[parts:]
    extras, refs = (refs[:parts], refs[parts:]) if added else ((), refs)
    gates, ups, downs, expand, refs = refs[0:2], refs[2:4], refs[4:6], refs[6], refs[7:]
    outs, refs = refs[:parts], refs[parts:]
    held, raised, sums, act, lowered, done = refs[:6]
    row_sem, meta_sem, raise_sem, lower_sem, out_sem = refs[6:11]
    size, width = rows[0].shape[0], rows[0].shape[1] - META
    hidden = sums.shape[1] // 2
    steps, tiles = width // DEPTH, width // TILE
    total = 2 * local * steps
    half = downs[0].shape[0]
    ahead = SLOTS - 1

    def row_copy(p, step):
        here = pl.ds(pl.multiple_of(step * DEPTH, DEPTH), DEPTH)
        return pltpu.make_async_copy(
            rows[p].at[:, here], held.at[pl.ds(p * size, size), here], row_sem.at[p, step]
        )

    def meta_copy(p):
        here = pl.ds(width, META)
        return pltpu.make_async_copy(
            rows[p].at[:, here], held.at[pl.ds(p * size, size), here], meta_sem.at[p]
        )

    def raise_copies(which, turn):
        slot, step = turn % SLOTS, turn % steps
        expert = turn // steps % local
        here = pl.ds(pl.multiple_of(step * DEPTH, DEPTH), DEPTH)
        return [
            pltpu.make_async_copy(
                source[which].at[expert, here, :],
                raised.at[slot, :, pl.ds(n * hidden, hidden)],
                raise_sem.at[slot, n],
            )
            for n, source in enumerate((gates, ups))
        ]

    def lower_copies(tile):
        slot = tile % SLOTS
        here = pl.ds(pl.multiple_of(tile * TILE, TILE), TILE)
        return [
            pltpu.make_async_copy(
                downs[n].at[:, here],
                lowered.at[slot, pl.ds(n * half, half), :],
                lower_sem.at[slot, n],
            )
            for n in range(2)
        ]

    def out_copies(tile):
        slot = tile % 2
        here = pl.ds(pl.multiple_of(tile * TILE, TILE), TILE)
        return [
            pltpu.make_async_copy(
                done.at[slot, pl.ds(p * size, size), :], outs[p].at[:, here], out_sem.at[slot, p]
            )
            for p in range(parts)
        ]

    def extra_copies(tile):
        joined, extra_sem = refs[11:]
        slot = tile % 2
        here = pl.ds(pl.multiple_of(tile * TILE, TILE), TILE)
        return [
            pltpu.make_async_copy(
                extras[p].at[:, here],
                joined.at[slot, pl.ds(p * size, size), :],
                extra_sem.at[slot, p],
            )
            for p in range(parts)
        ]

    def start_raise(turn):
        for which in range(2):

            @pl.when(turn // (steps * local) == which)
            def _():
                for copy in raise_copies(which, turn):
                    copy.start()

    def start_lower(tile):
        for copy in lower_copies(tile):
            copy.start()

    for p in range(parts):
        row_copy(p, 0).start()
    for copy in raise_copies(0, 0):
        copy.start()
    for p in range(parts):
        meta_copy(p).start()
    for turn in range(1, ahead):
        for copy in raise_copies(0, turn):
            copy.start()
        for p in range(parts):
            row_copy(p, turn).start()
    for step in range(ahead, steps):
        for p in range(parts):
            row_copy(p, step).start()

    @pl.loop(0, total)
    def _(turn):
        step, expert = turn % steps, turn // steps
        later = turn + ahead

        @pl.when(later < total)
        def _():
            start_raise(later)

        @pl.when(later >= total)
        def _():
            start_lower(later - total)

        @pl.when(turn < steps)
        def _():
            for p in range(parts):
                row_copy(p, step).wait()

        @pl.when(turn == 0)
        def _():
            for p in range(parts):
                meta_copy(p).wait()

        for copy in raise_copies(0, turn):
            copy.wait()
        slot = turn % SLOTS
        block = held[:, pl.ds(pl.multiple_of(step * DEPTH, DEPTH), DEPTH)]
        both = jnp.dot(block, raised[slot], preferred_element_type=jnp.float32)

        @pl.when(step == 0)
        def _():
            sums[...] = both

        @pl.when(step > 0)
        def _():
            sums[...] += both

        @pl.when(step == steps - 1)
        def _():
            mine = pl.ds(pl.multiple_of(expert * hidden, hidden), hidden)
            share = jnp.dot(
                held[:, width:], expand[:, mine], preferred_element_type=jnp.float32
            )
            gate, up = sums[:, :hidden], sums[:, hidden:]
            act[:, mine] = (gate / (1.0 + jnp.exp(-gate)) * up * share).astype(act.dtype)

    if added:
        for tile in range(2):
            for copy in extra_copies(tile):
                copy.start()

    @pl.loop(0, tiles)
    def _(tile):
        @pl.when(tile + ahead < tiles)
        def _():
            start_lower(tile + ahead)

        for copy in lower_copies(tile):
            copy.wait()

        @pl.when(tile >= 2)
        def _():
            for copy in out_copies(tile - 2):
                copy.wait()

        result = jnp.dot(act[...], lowered[tile % SLOTS], preferred_element_type=jnp.float32)
        if added:
            for copy in extra_copies(tile):
                copy.wait()
            result += refs[11][tile % 2].astype(jnp.float32)

            @pl.when(tile + 2 < tiles)
            def _():
                for copy in extra_copies(tile + 2):
                    copy.start()

        done[tile % 2] = result.astype(done.dtype)
        for copy in out_copies(tile):
            copy.start()

    for tile in range(tiles - 2, tiles):
        for copy in out_copies(tile):
            copy.wait()


def experts_of(pieces, gates, ups, downs, expand, extras=()):
    size, wide = pieces[0].shape
    local, width, hidden = gates[0].shape
    parts = len(pieces)
    count, inner = parts * size, 2 * local * hidden
    anywhere = pl.BlockSpec(memory_space=pl.ANY)
    return pl.pallas_call(
        functools.partial(experts_kernel, local, bool(extras)),
        out_shape=[jax.ShapeDtypeStruct((size, width), jnp.bfloat16)] * parts,
        in_specs=[anywhere] * (parts + len(extras) + 6) + [pl.BlockSpec(memory_space=pltpu.VMEM)],
        out_specs=[anywhere] * parts,
        scratch_shapes=[
            pltpu.VMEM((count, wide), jnp.bfloat16),
            pltpu.VMEM((SLOTS, DEPTH, 2 * hidden), jnp.bfloat16),
            pltpu.VMEM((count, 2 * hidden), jnp.float32),
            pltpu.VMEM((count, inner), jnp.bfloat16),
            pltpu.VMEM((SLOTS, inner, TILE), jnp.bfloat16),
            pltpu.VMEM((2, count, TILE), jnp.bfloat16),
            pltpu.SemaphoreType.DMA((parts, width // DEPTH)),
            pltpu.SemaphoreType.DMA((parts,)),
            pltpu.SemaphoreType.DMA((SLOTS, 2)),
            pltpu.SemaphoreType.DMA((SLOTS, 2)),
            pltpu.SemaphoreType.DMA((2, parts)),
        ]
        + [
            pltpu.VMEM((2, count, TILE), jnp.bfloat16),
            pltpu.SemaphoreType.DMA((2, parts)),
        ]
        * bool(extras),
        compiler_params=pltpu.CompilerParams(vmem_limit_bytes=VMEM_LIMIT),
        cost_estimate=pl.CostEstimate(
            flops=6 * count * width * inner,
            bytes_accessed=6 * width * inner + 4 * count * wide,
            transcendentals=count * inner,
        ),
        name="experts",
    )(*pieces, *extras, *gates, *ups, *downs, expand)


def together(*values):
    return lax.optimization_barrier(values)


def spread_weights(ids, weights, experts):
    hits = ids[:, :, None] == jnp.arange(experts, dtype=jnp.int32)[None, None, :]
    table = jnp.sum(jnp.where(hits, weights[:, :, None], 0.0), axis=1)
    high = table.astype(jnp.bfloat16)
    low = (table - high.astype(jnp.float32)).astype(jnp.bfloat16)
    return jnp.concatenate([high, low], axis=1)


def normalize(rows, gain):
    values = rows.astype(jnp.float32)
    factor = lax.rsqrt(jnp.mean(values * values, axis=-1, keepdims=True) + 1e-06)
    return (values * factor * gain).astype(jnp.bfloat16)


def pack_module(normed, accepted, owner_map, owners):
    count = normed.shape[0]
    requests = accepted.shape[0]
    per_request = count // requests
    capacity = 2 * per_request
    position = jnp.arange(count, dtype=jnp.int32)
    request = position // per_request
    place = position % per_request
    sizes = accepted + 1
    same = owner_map[:, None] == owner_map[None, :]
    earlier = (
        jnp.arange(requests, dtype=jnp.int32)[:, None]
        > jnp.arange(requests, dtype=jnp.int32)[None, :]
    )
    start = jnp.sum(jnp.where(same & earlier, sizes[None, :], 0), axis=1)
    live = place <= accepted[request]
    target = owner_map[request] * capacity + start[request] + place
    choose = (target[None, :] == jnp.arange(owners * capacity, dtype=jnp.int32)[:, None]) & live[
        None, :
    ]
    packed = jnp.dot(
        choose.astype(jnp.bfloat16), normed, preferred_element_type=jnp.float32
    ).astype(jnp.bfloat16)
    return packed.reshape(owners, capacity, normed.shape[1])


def body(
    hidden_rows,
    expert_ids,
    gate_weights,
    gate_matrix,
    up_matrix,
    down_matrix,
    module_gain,
    accepted,
    owner_map,
):
    owners = lax.axis_size("expert")
    local, width, hidden = gate_matrix.shape
    experts = local * owners
    count = hidden_rows.shape[0]
    parts = len(ORDERS)
    part = count // parts

    meta = spread_weights(expert_ids, gate_weights, experts)
    wide = jnp.concatenate([hidden_rows, meta], axis=1)

    mine = lax.axis_index("expert")
    column = jnp.arange(2 * local * hidden, dtype=jnp.int32) // hidden
    named = jnp.where(column < local, mine * local + column, (mine ^ 1) * local + column - local)
    expand = (
        jnp.arange(META, dtype=jnp.int32)[:, None] % experts == named[None, :]
    ).astype(jnp.bfloat16)

    blocks = [wide[p * part : (p + 1) * part] for p in range(parts)]
    for phase in (0, 1):
        for link in (0, 1):
            got = [swap(block, order[phase], link) for block, order in zip(blocks, ORDERS)]
            blocks, got = together(blocks, got)
            blocks = [jnp.concatenate(pair, axis=0) for pair in zip(blocks, got)]

    def outputs(pieces, extras=()):
        return experts_of(pieces, gates, ups, downs, expand, extras)

    def swap_last(values, link):
        return [swap(value, order[2], link) for value, order in zip(values, ORDERS)]

    def add(*values):
        return sum(value.astype(jnp.float32) for value in values)

    down_rows = down_matrix.reshape(local * hidden, width)
    near = swap_last(blocks, 0)
    gates = (gate_matrix, from_sibling(gate_matrix))
    ups = (up_matrix, from_sibling(up_matrix))
    near, blocks, gates, ups, down_rows = together(near, blocks, gates, ups, down_rows)
    following = swap_last(blocks, 1)
    downs = (down_rows, from_sibling(down_rows))
    following, near, downs = together(following, near, downs)
    across = swap_last(near, 1)
    out_following = outputs(following)
    across, out_following = together(across, out_following)
    from_following = swap_last(out_following, 1)
    out_across = outputs(across)
    from_following, out_across, near = together(from_following, out_across, near)
    for_near = swap_last(out_across, 1)
    out_near = outputs(near)
    for_near, out_near, blocks = together(for_near, out_near, blocks)
    for_near = [add(a, b).astype(jnp.bfloat16) for a, b in zip(out_near, for_near)]
    from_near = swap_last(for_near, 0)
    kept = outputs(blocks, from_following)
    terms = list(zip(kept, from_near))
    for phase in (1, 0):
        for link in (1, 0):
            half = terms[0][0].shape[0] // 2
            sent = [add(*[t[half:] for t in ts]).astype(jnp.bfloat16) for ts in terms]
            got = [swap(value, order[phase], link) for value, order in zip(sent, ORDERS)]
            kept = [add(*[t[:half] for t in ts]) for ts in terms]
            kept, got = together(kept, got)
            terms = list(zip(kept, got))
    update = jnp.concatenate([add(*ts) for ts in terms], axis=0)

    final_rows = (hidden_rows.astype(jnp.float32) + update).astype(jnp.bfloat16)
    normed = normalize(final_rows, module_gain)
    packed = pack_module(normed, accepted, owner_map, owners)
    shape = packed.shape
    packed = packed.reshape(owners, -1, LANES)
    delivered = lax.all_to_all(packed, "expert", split_axis=0, concat_axis=0, tiled=True)
    return (final_rows, delivered.reshape(1, 1, *shape))


def solution(mesh):
    return jax.shard_map(
        body,
        mesh=mesh,
        in_specs=(
            P(("dp", "expert"), None),
            P(("dp", "expert"), None),
            P(("dp", "expert"), None),
            P("expert", None, "dp"),
            P("expert", None, "dp"),
            P("expert", "dp", None),
            P(),
            P(("dp", "expert")),
            P(("dp", "expert")),
        ),
        out_specs=(P(("dp", "expert"), None), P("dp", "expert", None, None, None)),
        check_vma=False,
    )
```

```python
import functools

import jax
import jax.numpy as jnp
from jax import lax
from jax.experimental import pallas as pl
from jax.experimental.pallas import tpu as pltpu
from jax.sharding import PartitionSpec as P

AXES = ("dp", "expert")
RING = 4
CORES = 2
STRIDE = {"y": 32, "x": 8, "z": 2}
ORDERS = (("z", "y", "x"), ("x", "z", "y"), ("y", "x", "z"))
META = 128
PIECES = 4
DEPTH = 3584
TILE = 1024
SLOTS = 3
LOWER_SLOTS = 3
SPLIT = 1
VMEM_LIMIT = 36 * 1024 * 1024


def swap(value, axis, link):
    stride = STRIDE[axis]
    pairs = []
    for device in range(RING ** 3 * CORES):
        place = device // stride % RING
        flip = 1 if device % CORES == link else 3
        pairs.append((device, device + ((place ^ flip) - place) * stride))
    return lax.ppermute(value, AXES, pairs)


def from_sibling(value):
    devices = RING ** 3 * CORES
    return lax.ppermute(value, AXES, [(device, device ^ 1) for device in range(devices)])


def experts_kernel(local, cores, added, *refs):
    parts = len(ORDERS)
    rows, refs = refs[:parts], refs[parts:]
    extras, refs = refs[: added * parts], refs[added * parts :]
    gates, ups, downs = refs[:cores], refs[cores : 2 * cores], refs[2 * cores : 3 * cores]
    expand, refs = refs[3 * cores], refs[3 * cores + 1 :]
    outs, refs = refs[:parts], refs[parts:]
    held, raised, sums, act, lowered, done = refs[:6]
    row_sem, meta_sem, first_sem, raise_sem, lower_sem, out_sem = refs[6:12]
    size, width = rows[0].shape[0], rows[0].shape[1] - META
    hidden = sums.shape[1] // 2
    steps, tiles = width // DEPTH, width // TILE
    total = cores * local * steps
    half = downs[0].shape[0]
    ahead, soon = SLOTS - 1, LOWER_SLOTS - 1

    small = DEPTH // SPLIT

    def row_copy(p, piece):
        here = pl.ds(piece * small, small)
        return pltpu.make_async_copy(
            rows[p].at[:, here], held.at[pl.ds(p * size, size), here], row_sem.at[p, piece]
        )

    def first_copies(piece):
        here = pl.ds(piece * small, small)
        return [
            pltpu.make_async_copy(
                source[0].at[0, here, :],
                raised.at[0, here, pl.ds(n * hidden, hidden)],
                first_sem.at[piece, n],
            )
            for n, source in enumerate((gates, ups))
        ]

    def meta_copy(p):
        here = pl.ds(width, META)
        return pltpu.make_async_copy(
            rows[p].at[:, here], held.at[pl.ds(p * size, size), here], meta_sem.at[p]
        )

    def raise_copies(which, turn):
        slot, step = turn % SLOTS, turn % steps
        expert = turn // steps % local
        here = pl.ds(pl.multiple_of(step * DEPTH, DEPTH), DEPTH)
        return [
            pltpu.make_async_copy(
                source[which].at[expert, here, :],
                raised.at[slot, :, pl.ds(n * hidden, hidden)],
                raise_sem.at[slot, n],
            )
            for n, source in enumerate((gates, ups))
        ]

    def lower_copies(tile):
        slot = tile % LOWER_SLOTS
        here = pl.ds(pl.multiple_of(tile * TILE, TILE), TILE)
        return [
            pltpu.make_async_copy(
                downs[n].at[:, here],
                lowered.at[slot, pl.ds(n * half, half), :],
                lower_sem.at[slot, n],
            )
            for n in range(cores)
        ]

    def out_copies(tile):
        slot = tile % 2
        here = pl.ds(pl.multiple_of(tile * TILE, TILE), TILE)
        return [
            pltpu.make_async_copy(
                done.at[slot, pl.ds(p * size, size), :], outs[p].at[:, here], out_sem.at[slot, p]
            )
            for p in range(parts)
        ]

    def extra_copies(tile):
        joined, extra_sem = refs[12:]
        slot = tile % 2
        here = pl.ds(pl.multiple_of(tile * TILE, TILE), TILE)
        return [
            pltpu.make_async_copy(
                extras[n * parts + p].at[:, here],
                joined.at[slot, n, pl.ds(p * size, size), :],
                extra_sem.at[slot, n, p],
            )
            for n in range(added)
            for p in range(parts)
        ]

    def start_raise(turn):
        for which in range(cores):

            @pl.when(turn // (steps * local) == which)
            def _():
                for copy in raise_copies(which, turn):
                    copy.start()

    def start_lower(tile):
        for copy in lower_copies(tile):
            copy.start()

    for piece in range(SPLIT):
        for p in range(parts):
            row_copy(p, piece).start()
        for copy in first_copies(piece):
            copy.start()
    for p in range(parts):
        meta_copy(p).start()
    for turn in range(1, ahead):
        for copy in raise_copies(0, turn):
            copy.start()
        for piece in range(turn * SPLIT, (turn + 1) * SPLIT):
            for p in range(parts):
                row_copy(p, piece).start()
    for piece in range(ahead * SPLIT, steps * SPLIT):
        for p in range(parts):
            row_copy(p, piece).start()

    @pl.loop(0, total)
    def _(turn):
        step, expert = turn % steps, turn // steps
        later = turn + ahead

        @pl.when(later < total)
        def _():
            start_raise(later)

        @pl.when(turn >= total - soon)
        def _():
            start_lower(turn - total + soon)

        for late in range(1, steps):

            @pl.when(turn == late)
            def _():
                for piece in range(late * SPLIT, (late + 1) * SPLIT):
                    for p in range(parts):
                        row_copy(p, piece).wait()

        @pl.when(turn == 0)
        def _():
            for piece in range(SPLIT):
                for p in range(parts):
                    row_copy(p, piece).wait()
                for copy in first_copies(piece):
                    copy.wait()
                here = pl.ds(piece * small, small)
                both = jnp.dot(
                    held[:, here], raised[0, here, :], preferred_element_type=jnp.float32
                )
                if piece == 0:
                    sums[...] = both
                else:
                    sums[...] += both
            for p in range(parts):
                meta_copy(p).wait()

        @pl.when(turn > 0)
        def _():
            for copy in raise_copies(0, turn):
                copy.wait()
            block = held[:, pl.ds(pl.multiple_of(step * DEPTH, DEPTH), DEPTH)]
            both = jnp.dot(block, raised[turn % SLOTS], preferred_element_type=jnp.float32)

            @pl.when(step == 0)
            def _():
                sums[...] = both

            @pl.when(step > 0)
            def _():
                sums[...] += both

        @pl.when(step == steps - 1)
        def _():
            mine = pl.ds(pl.multiple_of(expert * hidden, hidden), hidden)
            share = jnp.dot(
                held[:, width:], expand[:, mine], preferred_element_type=jnp.float32
            )
            gate, up = sums[:, :hidden], sums[:, hidden:]
            act[:, mine] = (gate / (1.0 + jnp.exp(-gate)) * up * share).astype(act.dtype)

    if added:
        for tile in range(2):
            for copy in extra_copies(tile):
                copy.start()

    @pl.loop(0, tiles)
    def _(tile):
        @pl.when(tile + soon < tiles)
        def _():
            start_lower(tile + soon)

        for copy in lower_copies(tile):
            copy.wait()

        @pl.when(tile >= 2)
        def _():
            for copy in out_copies(tile - 2):
                copy.wait()

        result = jnp.dot(act[...], lowered[tile % LOWER_SLOTS], preferred_element_type=jnp.float32)
        if added:
            for copy in extra_copies(tile):
                copy.wait()
            for n in range(added):
                result += refs[12][tile % 2, n].astype(jnp.float32)

            @pl.when(tile + 2 < tiles)
            def _():
                for copy in extra_copies(tile + 2):
                    copy.start()

        done[tile % 2] = result.astype(done.dtype)
        for copy in out_copies(tile):
            copy.start()

    for tile in range(tiles - 2, tiles):
        for copy in out_copies(tile):
            copy.wait()


def experts_of(pieces, gates, ups, downs, expand, *extras):
    size, wide = pieces[0].shape
    local, width, hidden = gates[0].shape
    parts = len(pieces)
    cores, added = len(gates), len(extras)
    count, inner = parts * size, cores * local * hidden
    anywhere = pl.BlockSpec(memory_space=pl.ANY)
    return pl.pallas_call(
        functools.partial(experts_kernel, local, cores, added),
        out_shape=[jax.ShapeDtypeStruct((size, width), jnp.bfloat16)] * parts,
        in_specs=[anywhere] * (parts * (1 + added) + 3 * cores) + [pl.BlockSpec(memory_space=pltpu.VMEM)],
        out_specs=[anywhere] * parts,
        scratch_shapes=[
            pltpu.VMEM((count, wide), jnp.bfloat16),
            pltpu.VMEM((SLOTS, DEPTH, 2 * hidden), jnp.bfloat16),
            pltpu.VMEM((count, 2 * hidden), jnp.float32),
            pltpu.VMEM((count, inner), jnp.bfloat16),
            pltpu.VMEM((LOWER_SLOTS, inner, TILE), jnp.bfloat16),
            pltpu.VMEM((2, count, TILE), jnp.bfloat16),
            pltpu.SemaphoreType.DMA((parts, width // DEPTH * SPLIT)),
            pltpu.SemaphoreType.DMA((parts,)),
            pltpu.SemaphoreType.DMA((SPLIT, 2)),
            pltpu.SemaphoreType.DMA((SLOTS, 2)),
            pltpu.SemaphoreType.DMA((LOWER_SLOTS, 2)),
            pltpu.SemaphoreType.DMA((2, parts)),
        ]
        + [
            pltpu.VMEM((2, added, count, TILE), jnp.bfloat16),
            pltpu.SemaphoreType.DMA((2, added, parts)),
        ]
        * bool(added),
        compiler_params=pltpu.CompilerParams(vmem_limit_bytes=VMEM_LIMIT),
        cost_estimate=pl.CostEstimate(
            flops=6 * count * width * inner,
            bytes_accessed=6 * width * inner + 4 * count * wide,
            transcendentals=count * inner,
        ),
        name="experts",
    )(*pieces, *[value for extra in extras for value in extra], *gates, *ups, *downs, expand)


def together(*values):
    return lax.optimization_barrier(values)


def spread_weights(ids, weights, experts):
    hits = ids[:, :, None] == jnp.arange(experts, dtype=jnp.int32)[None, None, :]
    table = jnp.sum(jnp.where(hits, weights[:, :, None], 0.0), axis=1)
    high = table.astype(jnp.bfloat16)
    low = (table - high.astype(jnp.float32)).astype(jnp.bfloat16)
    return jnp.concatenate([high, low], axis=1)


def normalize(rows, gain):
    values = rows.astype(jnp.float32)
    factor = lax.rsqrt(jnp.mean(values * values, axis=-1, keepdims=True) + 1e-06)
    return (values * factor * gain).astype(jnp.bfloat16)


def pack_module(normed, accepted, owner_map, owners):
    count = normed.shape[0]
    requests = accepted.shape[0]
    per_request = count // requests
    capacity = 2 * per_request
    position = jnp.arange(count, dtype=jnp.int32)
    request = position // per_request
    place = position % per_request
    sizes = accepted + 1
    same = owner_map[:, None] == owner_map[None, :]
    earlier = (
        jnp.arange(requests, dtype=jnp.int32)[:, None]
        > jnp.arange(requests, dtype=jnp.int32)[None, :]
    )
    start = jnp.sum(jnp.where(same & earlier, sizes[None, :], 0), axis=1)
    live = place <= accepted[request]
    target = owner_map[request] * capacity + start[request] + place
    target = (target[:, None] * PIECES + jnp.arange(PIECES, dtype=jnp.int32)[None, :]).reshape(-1)
    live = jnp.repeat(live, PIECES)
    places = jnp.arange(owners * capacity * PIECES, dtype=jnp.int32)
    choose = (target[None, :] == places[:, None]) & live[None, :]
    packed = jnp.dot(
        choose.astype(jnp.bfloat16),
        normed.reshape(count * PIECES, -1),
        preferred_element_type=jnp.float32,
    ).astype(jnp.bfloat16)
    return packed.reshape(owners, capacity * PIECES, -1)


def unpack_kernel(owners, flat, out):
    count, width = out.shape[0], flat.shape[0]
    row = lax.broadcasted_iota(jnp.int32, (count, width), 0)
    column = lax.broadcasted_iota(jnp.int32, (count, width), 1)
    capacity = count // owners
    wanted = (row % owners * capacity + row // owners) * PIECES + pl.program_id(0)
    pick = jnp.where(column == wanted, 1.0, 0.0).astype(jnp.bfloat16)
    out[...] = jnp.dot(pick, flat[...], preferred_element_type=jnp.float32).astype(out.dtype)


def unpack(delivered):
    owners, pieces, width = delivered.shape
    capacity = pieces // PIECES
    count = owners * capacity
    rows = pl.pallas_call(
        functools.partial(unpack_kernel, owners),
        grid=(PIECES,),
        out_shape=jax.ShapeDtypeStruct((count, PIECES * width), jnp.bfloat16),
        in_specs=[pl.BlockSpec((owners * pieces, width), lambda q: (0, 0))],
        out_specs=pl.BlockSpec((count, width), lambda q: (0, q)),
        compiler_params=pltpu.CompilerParams(vmem_limit_bytes=VMEM_LIMIT),
        name="unpack",
    )(delivered.reshape(owners * pieces, width))
    return rows.reshape(capacity, owners, -1).transpose(1, 0, 2)


def body(
    hidden_rows,
    expert_ids,
    gate_weights,
    gate_matrix,
    up_matrix,
    down_matrix,
    module_gain,
    accepted,
    owner_map,
):
    owners = lax.axis_size("expert")
    local, width, hidden = gate_matrix.shape
    experts = local * owners
    count = hidden_rows.shape[0]
    parts = len(ORDERS)
    part = count // parts

    meta = spread_weights(expert_ids, gate_weights, experts)
    wide = jnp.concatenate([hidden_rows, meta], axis=1)

    here = lax.axis_index("expert")
    column = jnp.arange(2 * local * hidden, dtype=jnp.int32) // hidden
    named = jnp.where(column < local, here * local + column, (here ^ 1) * local + column - local)
    expand = (
        jnp.arange(META, dtype=jnp.int32)[:, None] % experts == named[None, :]
    ).astype(jnp.bfloat16)

    blocks = [wide[p * part : (p + 1) * part] for p in range(parts)]
    down_rows = down_matrix.reshape(local * hidden, width)
    for phase in (0, 1):
        for link in (0, 1):
            got = [swap(block, order[phase], link) for block, order in zip(blocks, ORDERS)]
            if (phase, link) == (1, 1):
                downs = (down_rows, from_sibling(down_rows))
                got, downs = together(got, downs)
            else:
                got, down_rows = together(got, down_rows)
            blocks = [jnp.concatenate(pair, axis=0) for pair in zip(blocks, got)]

    def outputs(pieces, *extras):
        return experts_of(pieces, gates, ups, downs, expand, *extras)

    def swap_last(values, link):
        return [swap(value, order[2], link) for value, order in zip(values, ORDERS)]

    def add(*values):
        return sum(value.astype(jnp.float32) for value in values)

    near = swap_last(blocks, 0)
    gates = (gate_matrix, from_sibling(gate_matrix))
    ups = (up_matrix, from_sibling(up_matrix))
    mine, other = expand[:, : local * hidden], expand[:, local * hidden :]
    out_own = experts_of(blocks, gates[:1], ups[:1], downs[:1], mine)
    near, blocks, gates, ups, out_own = together(near, blocks, gates, ups, out_own)
    following = swap_last(blocks, 1)
    out_near = outputs(near)
    following, near, out_near = together(following, near, out_near)
    across = swap_last(near, 1)
    out_following = outputs(following)
    across, out_following = together(across, out_following)
    from_following = swap_last(out_following, 1)
    out_across = outputs(across)
    from_following, out_across, blocks = together(from_following, out_across, blocks)
    for_near = swap_last(out_across, 1)
    for_near, blocks, out_near = together(for_near, blocks, out_near)
    for_near = [add(a, b).astype(jnp.bfloat16) for a, b in zip(out_near, for_near)]
    from_near = swap_last(for_near, 0)
    own = experts_of(blocks, gates[1:], ups[1:], downs[1:], other, from_following, out_own)
    from_near, own = together(from_near, own)
    left, got = own, from_near
    for phase, link in ((1, 1), (1, 0), (0, 1), (0, 0)):
        half = left[0].shape[0] // 2
        sent = [add(t[half:], g[half:]).astype(jnp.bfloat16) for t, g in zip(left, got)]
        left = [add(t[:half], g[:half]) for t, g in zip(left, got)]
        got = [swap(value, order[phase], link) for value, order in zip(sent, ORDERS)]
        left, got = together(left, got)
    update = jnp.concatenate([add(*ts) for ts in zip(left, got)], axis=0)

    final_rows = (hidden_rows.astype(jnp.float32) + update).astype(jnp.bfloat16)
    normed = normalize(final_rows, module_gain)
    packed = pack_module(normed, accepted, owner_map, owners)
    delivered = lax.all_to_all(packed, "expert", split_axis=0, concat_axis=0, tiled=True)
    return (final_rows, unpack(delivered)[None, None])


def solution(mesh):
    return jax.shard_map(
        body,
        mesh=mesh,
        in_specs=(
            P(("dp", "expert"), None),
            P(("dp", "expert"), None),
            P(("dp", "expert"), None),
            P("expert", None, "dp"),
            P("expert", None, "dp"),
            P("expert", "dp", None),
            P(),
            P(("dp", "expert")),
            P(("dp", "expert")),
        ),
        out_specs=(P(("dp", "expert"), None), P("dp", "expert", None, None, None)),
        check_vma=False,
    )
```

```python
import functools

import jax
import jax.numpy as jnp
from jax import lax
from jax.experimental import pallas as pl
from jax.experimental.pallas import tpu as pltpu
from jax.sharding import PartitionSpec as P

AXES = ("dp", "expert")
RING = 4
CORES = 2
STRIDE = {"y": 32, "x": 8, "z": 2}
ORDERS = (("z", "y", "x"), ("x", "z", "y"), ("y", "x", "z"))
META = 128
PIECES = 4
DEPTH = 3584
TILE = 1792
SLOTS = 3
LOWER_SLOTS = 3
SPLIT = 1
VMEM_LIMIT = 46 * 1024 * 1024


def swap(value, axis, link):
    stride = STRIDE[axis]
    pairs = []
    for device in range(RING ** 3 * CORES):
        place = device // stride % RING
        flip = 1 if device % CORES == link else 3
        pairs.append((device, device + ((place ^ flip) - place) * stride))
    return lax.ppermute(value, AXES, pairs)


def from_sibling(value):
    devices = RING ** 3 * CORES
    return lax.ppermute(value, AXES, [(device, device ^ 1) for device in range(devices)])


def experts_kernel(local, cores, added, *refs):
    parts = len(ORDERS)
    rows, refs = refs[:parts], refs[parts:]
    extras, refs = refs[: added * parts], refs[added * parts :]
    gates, ups, downs = refs[:cores], refs[cores : 2 * cores], refs[2 * cores : 3 * cores]
    expand, refs = refs[3 * cores], refs[3 * cores + 1 :]
    outs, refs = refs[:parts], refs[parts:]
    held, raised, sums, act, lowered, done = refs[:6]
    row_sem, meta_sem, first_sem, raise_sem, lower_sem, out_sem = refs[6:12]
    size, width = rows[0].shape[0], rows[0].shape[1] - META
    hidden = sums.shape[1] // 2
    steps, tiles = width // DEPTH, width // TILE
    total = cores * local * steps
    half = downs[0].shape[0]
    ahead, soon = SLOTS - 1, LOWER_SLOTS - 1

    small = DEPTH // SPLIT

    def row_copy(p, piece):
        here = pl.ds(piece * small, small)
        return pltpu.make_async_copy(
            rows[p].at[:, here], held.at[pl.ds(p * size, size), here], row_sem.at[p, piece]
        )

    def first_copies(piece):
        here = pl.ds(piece * small, small)
        return [
            pltpu.make_async_copy(
                source[0].at[0, here, :],
                raised.at[0, here, pl.ds(n * hidden, hidden)],
                first_sem.at[piece, n],
            )
            for n, source in enumerate((gates, ups))
        ]

    def meta_copy(p):
        here = pl.ds(width, META)
        return pltpu.make_async_copy(
            rows[p].at[:, here], held.at[pl.ds(p * size, size), here], meta_sem.at[p]
        )

    def raise_copies(which, turn):
        slot, step = turn % SLOTS, turn % steps
        expert = turn // steps % local
        here = pl.ds(pl.multiple_of(step * DEPTH, DEPTH), DEPTH)
        return [
            pltpu.make_async_copy(
                source[which].at[expert, here, :],
                raised.at[slot, :, pl.ds(n * hidden, hidden)],
                raise_sem.at[slot, n],
            )
            for n, source in enumerate((gates, ups))
        ]

    def lower_copies(tile):
        slot = tile % LOWER_SLOTS
        here = pl.ds(pl.multiple_of(tile * TILE, TILE), TILE)
        return [
            pltpu.make_async_copy(
                downs[n].at[:, here],
                lowered.at[slot, pl.ds(n * half, half), :],
                lower_sem.at[slot, n],
            )
            for n in range(cores)
        ]

    def out_copies(tile):
        slot = tile % 2
        here = pl.ds(pl.multiple_of(tile * TILE, TILE), TILE)
        return [
            pltpu.make_async_copy(
                done.at[slot, pl.ds(p * size, size), :], outs[p].at[:, here], out_sem.at[slot, p]
            )
            for p in range(parts)
        ]

    def extra_copies(tile):
        joined, extra_sem = refs[12:]
        slot = tile % 2
        here = pl.ds(pl.multiple_of(tile * TILE, TILE), TILE)
        return [
            pltpu.make_async_copy(
                extras[n * parts + p].at[:, here],
                joined.at[slot, n, pl.ds(p * size, size), :],
                extra_sem.at[slot, n, p],
            )
            for n in range(added)
            for p in range(parts)
        ]

    def start_raise(turn):
        for which in range(cores):

            @pl.when(turn // (steps * local) == which)
            def _():
                for copy in raise_copies(which, turn):
                    copy.start()

    def start_lower(tile):
        for copy in lower_copies(tile):
            copy.start()

    for piece in range(SPLIT):
        for p in range(parts):
            row_copy(p, piece).start()
        for copy in first_copies(piece):
            copy.start()
    for p in range(parts):
        meta_copy(p).start()
    for turn in range(1, ahead):
        for copy in raise_copies(0, turn):
            copy.start()
        for piece in range(turn * SPLIT, (turn + 1) * SPLIT):
            for p in range(parts):
                row_copy(p, piece).start()
    for piece in range(ahead * SPLIT, steps * SPLIT):
        for p in range(parts):
            row_copy(p, piece).start()

    @pl.loop(0, total)
    def _(turn):
        step, expert = turn % steps, turn // steps
        later = turn + ahead

        @pl.when(later < total)
        def _():
            start_raise(later)

        @pl.when(turn >= total - soon)
        def _():
            start_lower(turn - total + soon)

        for late in range(1, steps):

            @pl.when(turn == late)
            def _():
                for piece in range(late * SPLIT, (late + 1) * SPLIT):
                    for p in range(parts):
                        row_copy(p, piece).wait()

        @pl.when(turn == 0)
        def _():
            for piece in range(SPLIT):
                for p in range(parts):
                    row_copy(p, piece).wait()
                for copy in first_copies(piece):
                    copy.wait()
                here = pl.ds(piece * small, small)
                both = jnp.dot(
                    held[:, here], raised[0, here, :], preferred_element_type=jnp.float32
                )
                if piece == 0:
                    sums[...] = both
                else:
                    sums[...] += both
            for p in range(parts):
                meta_copy(p).wait()

        @pl.when(turn > 0)
        def _():
            for copy in raise_copies(0, turn):
                copy.wait()
            block = held[:, pl.ds(pl.multiple_of(step * DEPTH, DEPTH), DEPTH)]
            both = jnp.dot(block, raised[turn % SLOTS], preferred_element_type=jnp.float32)

            @pl.when(step == 0)
            def _():
                sums[...] = both

            @pl.when(step > 0)
            def _():
                sums[...] += both

        @pl.when(step == steps - 1)
        def _():
            mine = pl.ds(pl.multiple_of(expert * hidden, hidden), hidden)
            share = jnp.dot(
                held[:, width:], expand[:, mine], preferred_element_type=jnp.float32
            )
            gate, up = sums[:, :hidden], sums[:, hidden:]
            act[:, mine] = (gate / (1.0 + jnp.exp(-gate)) * up * share).astype(act.dtype)

    if added:
        for tile in range(2):
            for copy in extra_copies(tile):
                copy.start()

    @pl.loop(0, tiles)
    def _(tile):
        @pl.when(tile + soon < tiles)
        def _():
            start_lower(tile + soon)

        for copy in lower_copies(tile):
            copy.wait()

        @pl.when(tile >= 2)
        def _():
            for copy in out_copies(tile - 2):
                copy.wait()

        result = jnp.dot(act[...], lowered[tile % LOWER_SLOTS], preferred_element_type=jnp.float32)
        if added:
            for copy in extra_copies(tile):
                copy.wait()
            for n in range(added):
                result += refs[12][tile % 2, n].astype(jnp.float32)

            @pl.when(tile + 2 < tiles)
            def _():
                for copy in extra_copies(tile + 2):
                    copy.start()

        done[tile % 2] = result.astype(done.dtype)
        for copy in out_copies(tile):
            copy.start()

    for tile in range(tiles - 2, tiles):
        for copy in out_copies(tile):
            copy.wait()


def experts_of(pieces, gates, ups, downs, expand, *extras):
    size, wide = pieces[0].shape
    local, width, hidden = gates[0].shape
    parts = len(pieces)
    cores, added = len(gates), len(extras)
    count, inner = parts * size, cores * local * hidden
    anywhere = pl.BlockSpec(memory_space=pl.ANY)
    return pl.pallas_call(
        functools.partial(experts_kernel, local, cores, added),
        out_shape=[jax.ShapeDtypeStruct((size, width), jnp.bfloat16)] * parts,
        in_specs=[anywhere] * (parts * (1 + added) + 3 * cores) + [pl.BlockSpec(memory_space=pltpu.VMEM)],
        out_specs=[anywhere] * parts,
        scratch_shapes=[
            pltpu.VMEM((count, wide), jnp.bfloat16),
            pltpu.VMEM((SLOTS, DEPTH, 2 * hidden), jnp.bfloat16),
            pltpu.VMEM((count, 2 * hidden), jnp.float32),
            pltpu.VMEM((count, inner), jnp.bfloat16),
            pltpu.VMEM((LOWER_SLOTS, inner, TILE), jnp.bfloat16),
            pltpu.VMEM((2, count, TILE), jnp.bfloat16),
            pltpu.SemaphoreType.DMA((parts, width // DEPTH * SPLIT)),
            pltpu.SemaphoreType.DMA((parts,)),
            pltpu.SemaphoreType.DMA((SPLIT, 2)),
            pltpu.SemaphoreType.DMA((SLOTS, 2)),
            pltpu.SemaphoreType.DMA((LOWER_SLOTS, 2)),
            pltpu.SemaphoreType.DMA((2, parts)),
        ]
        + [
            pltpu.VMEM((2, added, count, TILE), jnp.bfloat16),
            pltpu.SemaphoreType.DMA((2, added, parts)),
        ]
        * bool(added),
        compiler_params=pltpu.CompilerParams(vmem_limit_bytes=VMEM_LIMIT),
        cost_estimate=pl.CostEstimate(
            flops=6 * count * width * inner,
            bytes_accessed=6 * width * inner + 4 * count * wide,
            transcendentals=count * inner,
        ),
        name="experts",
    )(*pieces, *[value for extra in extras for value in extra], *gates, *ups, *downs, expand)


def together(*values):
    return lax.optimization_barrier(values)


def in_step(values):
    pulse = from_sibling(values[-1][:8, :128])
    values, pulse = together(values, pulse)
    return values, pulse[0, 0].astype(jnp.float32)


def spread_weights(ids, weights, experts):
    hits = ids[:, :, None] == jnp.arange(experts, dtype=jnp.int32)[None, None, :]
    table = jnp.sum(jnp.where(hits, weights[:, :, None], 0.0), axis=1)
    high = table.astype(jnp.bfloat16)
    low = (table - high.astype(jnp.float32)).astype(jnp.bfloat16)
    return jnp.concatenate([high, low], axis=1)


def normalize(rows, gain):
    values = rows.astype(jnp.float32)
    factor = lax.rsqrt(jnp.mean(values * values, axis=-1, keepdims=True) + 1e-06)
    return (values * factor * gain).astype(jnp.bfloat16)


def pack_module(normed, accepted, owner_map, owners):
    count = normed.shape[0]
    requests = accepted.shape[0]
    per_request = count // requests
    capacity = 2 * per_request
    position = jnp.arange(count, dtype=jnp.int32)
    request = position // per_request
    place = position % per_request
    sizes = accepted + 1
    same = owner_map[:, None] == owner_map[None, :]
    earlier = (
        jnp.arange(requests, dtype=jnp.int32)[:, None]
        > jnp.arange(requests, dtype=jnp.int32)[None, :]
    )
    start = jnp.sum(jnp.where(same & earlier, sizes[None, :], 0), axis=1)
    live = place <= accepted[request]
    target = owner_map[request] * capacity + start[request] + place
    target = (target[:, None] * PIECES + jnp.arange(PIECES, dtype=jnp.int32)[None, :]).reshape(-1)
    live = jnp.repeat(live, PIECES)
    places = jnp.arange(owners * capacity * PIECES, dtype=jnp.int32)
    choose = (target[None, :] == places[:, None]) & live[None, :]
    packed = jnp.dot(
        choose.astype(jnp.bfloat16),
        normed.reshape(count * PIECES, -1),
        preferred_element_type=jnp.float32,
    ).astype(jnp.bfloat16)
    return packed.reshape(owners, capacity * PIECES, -1)


def unpack_kernel(owners, flat, out):
    count, width = out.shape[0], flat.shape[0]
    row = lax.broadcasted_iota(jnp.int32, (count, width), 0)
    column = lax.broadcasted_iota(jnp.int32, (count, width), 1)
    capacity = count // owners
    wanted = (row % owners * capacity + row // owners) * PIECES + pl.program_id(0)
    pick = jnp.where(column == wanted, 1.0, 0.0).astype(jnp.bfloat16)
    out[...] = jnp.dot(pick, flat[...], preferred_element_type=jnp.float32).astype(out.dtype)


def unpack(delivered):
    owners, pieces, width = delivered.shape
    capacity = pieces // PIECES
    count = owners * capacity
    rows = pl.pallas_call(
        functools.partial(unpack_kernel, owners),
        grid=(PIECES,),
        out_shape=jax.ShapeDtypeStruct((count, PIECES * width), jnp.bfloat16),
        in_specs=[pl.BlockSpec((owners * pieces, width), lambda q: (0, 0))],
        out_specs=pl.BlockSpec((count, width), lambda q: (0, q)),
        compiler_params=pltpu.CompilerParams(vmem_limit_bytes=VMEM_LIMIT),
        name="unpack",
    )(delivered.reshape(owners * pieces, width))
    return rows.reshape(capacity, owners, -1).transpose(1, 0, 2)


def body(
    hidden_rows,
    expert_ids,
    gate_weights,
    gate_matrix,
    up_matrix,
    down_matrix,
    module_gain,
    accepted,
    owner_map,
):
    owners = lax.axis_size("expert")
    local, width, hidden = gate_matrix.shape
    experts = local * owners
    count = hidden_rows.shape[0]
    parts = len(ORDERS)
    part = count // parts

    meta = spread_weights(expert_ids, gate_weights, experts)
    wide = jnp.concatenate([hidden_rows, meta], axis=1)

    here = lax.axis_index("expert")
    column = jnp.arange(2 * local * hidden, dtype=jnp.int32) // hidden
    named = jnp.where(column < local, here * local + column, (here ^ 1) * local + column - local)
    expand = (
        jnp.arange(META, dtype=jnp.int32)[:, None] % experts == named[None, :]
    ).astype(jnp.bfloat16)

    blocks = [wide[p * part : (p + 1) * part] for p in range(parts)]
    down_rows = down_matrix.reshape(local * hidden, width)
    for phase in (0, 1):
        for link in (0, 1):
            got = [swap(block, order[phase], link) for block, order in zip(blocks, ORDERS)]
            if (phase, link) == (1, 1):
                downs = (down_rows, from_sibling(down_rows))
                blocks, got, downs = together(blocks, got, downs)
            else:
                blocks, got, down_rows = together(blocks, got, down_rows)
            blocks = [jnp.concatenate(pair, axis=0) for pair in zip(blocks, got)]

    def outputs(pieces, *extras):
        return experts_of(pieces, gates, ups, downs, expand, *extras)

    def swap_last(values, link):
        return [swap(value, order[2], link) for value, order in zip(values, ORDERS)]

    def add(*values):
        return sum(value.astype(jnp.float32) for value in values)

    near = swap_last(blocks, 0)
    gates = (gate_matrix, from_sibling(gate_matrix))
    ups = (up_matrix, from_sibling(up_matrix))
    near, blocks, gates, ups = together(near, blocks, gates, ups)
    following = swap_last(blocks, 1)
    out_near = outputs(near)
    following, near, out_near = together(following, near, out_near)
    across = swap_last(near, 1)
    out_following = outputs(following)
    across, out_following = together(across, out_following)
    from_following = swap_last(out_following, 1)
    out_across = outputs(across)
    from_following, out_across, blocks = together(from_following, out_across, blocks)
    for_near = swap_last(out_across, 1)
    own = outputs(blocks, from_following)
    for_near, own, out_near = together(for_near, own, out_near)
    for_near = [add(a, b).astype(jnp.bfloat16) for a, b in zip(out_near, for_near)]
    for_near, pulse = in_step(for_near)
    from_near = swap_last(for_near, 0)
    from_near, own = together(from_near, own)
    from_near, other_pulse = in_step(from_near)
    pulse = 0.0 * (pulse + other_pulse)
    left, got = own, from_near
    for phase, link in ((1, 1), (1, 0), (0, 1), (0, 0)):
        half = left[0].shape[0] // 2
        sent = [add(t[half:], g[half:]).astype(jnp.bfloat16) for t, g in zip(left, got)]
        left = [add(t[:half], g[:half]).astype(jnp.bfloat16) for t, g in zip(left, got)]
        got = [swap(value, order[phase], link) for value, order in zip(sent, ORDERS)]
        left, got = together(left, got)
    update = jnp.concatenate([add(*ts) for ts in zip(left, got)], axis=0)

    final_rows = (hidden_rows.astype(jnp.float32) + update).astype(jnp.bfloat16)
    normed = normalize(final_rows, module_gain + pulse)
    packed = pack_module(normed, accepted, owner_map, owners)
    delivered = lax.all_to_all(packed, "expert", split_axis=0, concat_axis=0, tiled=True)
    return (final_rows, unpack(delivered)[None, None])


def solution(mesh):
    return jax.shard_map(
        body,
        mesh=mesh,
        in_specs=(
            P(("dp", "expert"), None),
            P(("dp", "expert"), None),
            P(("dp", "expert"), None),
            P("expert", None, "dp"),
            P("expert", None, "dp"),
            P("expert", "dp", None),
            P(),
            P(("dp", "expert")),
            P(("dp", "expert")),
        ),
        out_specs=(P(("dp", "expert"), None), P("dp", "expert", None, None, None)),
        check_vma=False,
    )
```

```python
import functools

import jax
import jax.numpy as jnp
from jax import lax
from jax.experimental import pallas as pl
from jax.experimental.pallas import tpu as pltpu
from jax.sharding import PartitionSpec as P

AXES = ("dp", "expert")
RING = 4
CORES = 2
STRIDE = {"y": 32, "x": 8, "z": 2}
ORDERS = (("z", "y", "x"), ("x", "z", "y"), ("y", "x", "z"))
META = 128
PIECES = 4
DEPTH = 3584
TILE = 1792
SLOTS = 3
LOWER_SLOTS = 3
SPLIT = 1
VMEM_LIMIT = 46 * 1024 * 1024


def swap(value, axis, link):
    stride = STRIDE[axis]
    pairs = []
    for device in range(RING ** 3 * CORES):
        place = device // stride % RING
        flip = 1 if device % CORES == link else 3
        pairs.append((device, device + ((place ^ flip) - place) * stride))
    return lax.ppermute(value, AXES, pairs)


def from_sibling(value):
    devices = RING ** 3 * CORES
    return lax.ppermute(value, AXES, [(device, device ^ 1) for device in range(devices)])


def experts_kernel(local, cores, added, *refs):
    parts = len(ORDERS)
    rows, refs = refs[:parts], refs[parts:]
    extras, refs = refs[: added * parts], refs[added * parts :]
    gates, ups, downs = refs[:cores], refs[cores : 2 * cores], refs[2 * cores : 3 * cores]
    expand, refs = refs[3 * cores], refs[3 * cores + 1 :]
    outs, refs = refs[:parts], refs[parts:]
    held, raised, sums, act, lowered, done = refs[:6]
    row_sem, meta_sem, first_sem, raise_sem, lower_sem, out_sem = refs[6:12]
    size, width = rows[0].shape[0], rows[0].shape[1] - META
    hidden = sums.shape[1] // 2
    steps, tiles = width // DEPTH, width // TILE
    total = cores * local * steps
    half = downs[0].shape[0]
    ahead, soon = SLOTS - 1, LOWER_SLOTS - 1

    small = DEPTH // SPLIT

    def row_copy(p, piece):
        here = pl.ds(piece * small, small)
        return pltpu.make_async_copy(
            rows[p].at[:, here], held.at[pl.ds(p * size, size), here], row_sem.at[p, piece]
        )

    def first_copies(piece):
        here = pl.ds(piece * small, small)
        return [
            pltpu.make_async_copy(
                source[0].at[0, here, :],
                raised.at[0, here, pl.ds(n * hidden, hidden)],
                first_sem.at[piece, n],
            )
            for n, source in enumerate((gates, ups))
        ]

    def meta_copy(p):
        here = pl.ds(width, META)
        return pltpu.make_async_copy(
            rows[p].at[:, here], held.at[pl.ds(p * size, size), here], meta_sem.at[p]
        )

    def raise_copies(which, turn):
        slot, step = turn % SLOTS, turn % steps
        expert = turn // steps % local
        here = pl.ds(pl.multiple_of(step * DEPTH, DEPTH), DEPTH)
        return [
            pltpu.make_async_copy(
                source[which].at[expert, here, :],
                raised.at[slot, :, pl.ds(n * hidden, hidden)],
                raise_sem.at[slot, n],
            )
            for n, source in enumerate((gates, ups))
        ]

    def lower_copies(tile):
        slot = tile % LOWER_SLOTS
        here = pl.ds(pl.multiple_of(tile * TILE, TILE), TILE)
        return [
            pltpu.make_async_copy(
                downs[n].at[:, here],
                lowered.at[slot, pl.ds(n * half, half), :],
                lower_sem.at[slot, n],
            )
            for n in range(cores)
        ]

    def out_copies(tile):
        slot = tile % 2
        here = pl.ds(pl.multiple_of(tile * TILE, TILE), TILE)
        return [
            pltpu.make_async_copy(
                done.at[slot, pl.ds(p * size, size), :], outs[p].at[:, here], out_sem.at[slot, p]
            )
            for p in range(parts)
        ]

    def extra_copies(tile):
        joined, extra_sem = refs[12:]
        slot = tile % 2
        here = pl.ds(pl.multiple_of(tile * TILE, TILE), TILE)
        return [
            pltpu.make_async_copy(
                extras[n * parts + p].at[:, here],
                joined.at[slot, n, pl.ds(p * size, size), :],
                extra_sem.at[slot, n, p],
            )
            for n in range(added)
            for p in range(parts)
        ]

    def start_raise(turn):
        for which in range(cores):

            @pl.when(turn // (steps * local) == which)
            def _():
                for copy in raise_copies(which, turn):
                    copy.start()

    def start_lower(tile):
        for copy in lower_copies(tile):
            copy.start()

    for piece in range(SPLIT):
        for p in range(parts):
            row_copy(p, piece).start()
        for copy in first_copies(piece):
            copy.start()
    for p in range(parts):
        meta_copy(p).start()
    for turn in range(1, ahead):
        for copy in raise_copies(0, turn):
            copy.start()
        for piece in range(turn * SPLIT, (turn + 1) * SPLIT):
            for p in range(parts):
                row_copy(p, piece).start()
    for piece in range(ahead * SPLIT, steps * SPLIT):
        for p in range(parts):
            row_copy(p, piece).start()

    @pl.loop(0, total)
    def _(turn):
        step, expert = turn % steps, turn // steps
        later = turn + ahead

        @pl.when(later < total)
        def _():
            start_raise(later)

        @pl.when(turn >= total - soon)
        def _():
            start_lower(turn - total + soon)

        for late in range(1, steps):

            @pl.when(turn == late)
            def _():
                for piece in range(late * SPLIT, (late + 1) * SPLIT):
                    for p in range(parts):
                        row_copy(p, piece).wait()

        @pl.when(turn == 0)
        def _():
            for piece in range(SPLIT):
                for p in range(parts):
                    row_copy(p, piece).wait()
                for copy in first_copies(piece):
                    copy.wait()
                here = pl.ds(piece * small, small)
                both = jnp.dot(
                    held[:, here], raised[0, here, :], preferred_element_type=jnp.float32
                )
                if piece == 0:
                    sums[...] = both
                else:
                    sums[...] += both
            for p in range(parts):
                meta_copy(p).wait()

        @pl.when(turn > 0)
        def _():
            for copy in raise_copies(0, turn):
                copy.wait()
            block = held[:, pl.ds(pl.multiple_of(step * DEPTH, DEPTH), DEPTH)]
            both = jnp.dot(block, raised[turn % SLOTS], preferred_element_type=jnp.float32)

            @pl.when(step == 0)
            def _():
                sums[...] = both

            @pl.when(step > 0)
            def _():
                sums[...] += both

        @pl.when(step == steps - 1)
        def _():
            mine = pl.ds(pl.multiple_of(expert * hidden, hidden), hidden)
            share = jnp.dot(
                held[:, width:], expand[:, mine], preferred_element_type=jnp.float32
            )
            gate, up = sums[:, :hidden], sums[:, hidden:]
            act[:, mine] = (gate / (1.0 + jnp.exp(-gate)) * up * share).astype(act.dtype)

    if added:
        for tile in range(2):
            for copy in extra_copies(tile):
                copy.start()

    @pl.loop(0, tiles)
    def _(tile):
        @pl.when(tile + soon < tiles)
        def _():
            start_lower(tile + soon)

        for copy in lower_copies(tile):
            copy.wait()

        @pl.when(tile >= 2)
        def _():
            for copy in out_copies(tile - 2):
                copy.wait()

        result = jnp.dot(act[...], lowered[tile % LOWER_SLOTS], preferred_element_type=jnp.float32)
        if added:
            for copy in extra_copies(tile):
                copy.wait()
            for n in range(added):
                result += refs[12][tile % 2, n].astype(jnp.float32)

            @pl.when(tile + 2 < tiles)
            def _():
                for copy in extra_copies(tile + 2):
                    copy.start()

        done[tile % 2] = result.astype(done.dtype)
        for copy in out_copies(tile):
            copy.start()

    for tile in range(tiles - 2, tiles):
        for copy in out_copies(tile):
            copy.wait()


def experts_of(pieces, gates, ups, downs, expand, *extras):
    size, wide = pieces[0].shape
    local, width, hidden = gates[0].shape
    parts = len(pieces)
    cores, added = len(gates), len(extras)
    count, inner = parts * size, cores * local * hidden
    anywhere = pl.BlockSpec(memory_space=pl.ANY)
    return pl.pallas_call(
        functools.partial(experts_kernel, local, cores, added),
        out_shape=[jax.ShapeDtypeStruct((size, width), jnp.bfloat16)] * parts,
        in_specs=[anywhere] * (parts * (1 + added) + 3 * cores) + [pl.BlockSpec(memory_space=pltpu.VMEM)],
        out_specs=[anywhere] * parts,
        scratch_shapes=[
            pltpu.VMEM((count, wide), jnp.bfloat16),
            pltpu.VMEM((SLOTS, DEPTH, 2 * hidden), jnp.bfloat16),
            pltpu.VMEM((count, 2 * hidden), jnp.float32),
            pltpu.VMEM((count, inner), jnp.bfloat16),
            pltpu.VMEM((LOWER_SLOTS, inner, TILE), jnp.bfloat16),
            pltpu.VMEM((2, count, TILE), jnp.bfloat16),
            pltpu.SemaphoreType.DMA((parts, width // DEPTH * SPLIT)),
            pltpu.SemaphoreType.DMA((parts,)),
            pltpu.SemaphoreType.DMA((SPLIT, 2)),
            pltpu.SemaphoreType.DMA((SLOTS, 2)),
            pltpu.SemaphoreType.DMA((LOWER_SLOTS, 2)),
            pltpu.SemaphoreType.DMA((2, parts)),
        ]
        + [
            pltpu.VMEM((2, added, count, TILE), jnp.bfloat16),
            pltpu.SemaphoreType.DMA((2, added, parts)),
        ]
        * bool(added),
        compiler_params=pltpu.CompilerParams(vmem_limit_bytes=VMEM_LIMIT),
        cost_estimate=pl.CostEstimate(
            flops=6 * count * width * inner,
            bytes_accessed=6 * width * inner + 4 * count * wide,
            transcendentals=count * inner,
        ),
        name="experts",
    )(*pieces, *[value for extra in extras for value in extra], *gates, *ups, *downs, expand)


def together(*values):
    return lax.optimization_barrier(values)


def in_step(values):
    pulse = from_sibling(values[-1][:8, :128])
    values, pulse = together(values, pulse)
    return values, pulse[0, 0].astype(jnp.float32)


def spread_weights(ids, weights, experts):
    hits = ids[:, :, None] == jnp.arange(experts, dtype=jnp.int32)[None, None, :]
    table = jnp.sum(jnp.where(hits, weights[:, :, None], 0.0), axis=1)
    high = table.astype(jnp.bfloat16)
    low = (table - high.astype(jnp.float32)).astype(jnp.bfloat16)
    return jnp.concatenate([high, low], axis=1)


def normalize(rows, gain):
    values = rows.astype(jnp.float32)
    factor = lax.rsqrt(jnp.mean(values * values, axis=-1, keepdims=True) + 1e-06)
    return (values * factor * gain).astype(jnp.bfloat16)


def pack_module(normed, accepted, owner_map, owners):
    count = normed.shape[0]
    requests = accepted.shape[0]
    per_request = count // requests
    capacity = 2 * per_request
    position = jnp.arange(count, dtype=jnp.int32)
    request = position // per_request
    place = position % per_request
    sizes = accepted + 1
    same = owner_map[:, None] == owner_map[None, :]
    earlier = (
        jnp.arange(requests, dtype=jnp.int32)[:, None]
        > jnp.arange(requests, dtype=jnp.int32)[None, :]
    )
    start = jnp.sum(jnp.where(same & earlier, sizes[None, :], 0), axis=1)
    live = place <= accepted[request]
    target = owner_map[request] * capacity + start[request] + place
    target = (target[:, None] * PIECES + jnp.arange(PIECES, dtype=jnp.int32)[None, :]).reshape(-1)
    live = jnp.repeat(live, PIECES)
    places = jnp.arange(owners * capacity * PIECES, dtype=jnp.int32)
    choose = (target[None, :] == places[:, None]) & live[None, :]
    packed = jnp.dot(
        choose.astype(jnp.bfloat16),
        normed.reshape(count * PIECES, -1),
        preferred_element_type=jnp.float32,
    ).astype(jnp.bfloat16)
    return packed.reshape(owners, capacity * PIECES, -1)


def unpack_kernel(owners, flat, out):
    count, width = out.shape[0], flat.shape[0]
    row = lax.broadcasted_iota(jnp.int32, (count, width), 0)
    column = lax.broadcasted_iota(jnp.int32, (count, width), 1)
    capacity = count // owners
    wanted = (row % owners * capacity + row // owners) * PIECES + pl.program_id(0)
    pick = jnp.where(column == wanted, 1.0, 0.0).astype(jnp.bfloat16)
    out[...] = jnp.dot(pick, flat[...], preferred_element_type=jnp.float32).astype(out.dtype)


def unpack(delivered):
    owners, pieces, width = delivered.shape
    capacity = pieces // PIECES
    count = owners * capacity
    rows = pl.pallas_call(
        functools.partial(unpack_kernel, owners),
        grid=(PIECES,),
        out_shape=jax.ShapeDtypeStruct((count, PIECES * width), jnp.bfloat16),
        in_specs=[pl.BlockSpec((owners * pieces, width), lambda q: (0, 0))],
        out_specs=pl.BlockSpec((count, width), lambda q: (0, q)),
        compiler_params=pltpu.CompilerParams(vmem_limit_bytes=VMEM_LIMIT),
        name="unpack",
    )(delivered.reshape(owners * pieces, width))
    return rows.reshape(capacity, owners, -1).transpose(1, 0, 2)


def body(
    hidden_rows,
    expert_ids,
    gate_weights,
    gate_matrix,
    up_matrix,
    down_matrix,
    module_gain,
    accepted,
    owner_map,
):
    owners = lax.axis_size("expert")
    local, width, hidden = gate_matrix.shape
    experts = local * owners
    count = hidden_rows.shape[0]
    parts = len(ORDERS)
    part = count // parts

    meta = spread_weights(expert_ids, gate_weights, experts)
    wide = jnp.concatenate([hidden_rows, meta], axis=1)

    here = lax.axis_index("expert")
    column = jnp.arange(2 * local * hidden, dtype=jnp.int32) // hidden
    named = jnp.where(column < local, here * local + column, (here ^ 1) * local + column - local)
    expand = (
        jnp.arange(META, dtype=jnp.int32)[:, None] % experts == named[None, :]
    ).astype(jnp.bfloat16)

    blocks = [wide[p * part : (p + 1) * part] for p in range(parts)]
    down_rows = down_matrix.reshape(local * hidden, width)
    for phase in (0, 1):
        for link in (0, 1):
            got = [swap(block, order[phase], link) for block, order in zip(blocks, ORDERS)]
            if (phase, link) == (1, 1):
                downs = (down_rows, from_sibling(down_rows))
                blocks, got, downs = together(blocks, got, downs)
            else:
                blocks, got, down_rows = together(blocks, got, down_rows)
            blocks = [jnp.concatenate(pair, axis=0) for pair in zip(blocks, got)]

    def outputs(pieces, *extras):
        return experts_of(pieces, gates, ups, downs, expand, *extras)

    def swap_last(values, link):
        return [swap(value, order[2], link) for value, order in zip(values, ORDERS)]

    def add(*values):
        return sum(value.astype(jnp.float32) for value in values)

    near = swap_last(blocks, 0)
    gates = (gate_matrix, from_sibling(gate_matrix))
    ups = (up_matrix, from_sibling(up_matrix))
    near, blocks, gates, ups = together(near, blocks, gates, ups)
    following = swap_last(blocks, 1)
    out_near = outputs(near)
    following, near, out_near = together(following, near, out_near)
    across = swap_last(near, 1)
    out_following = outputs(following)
    across, out_following = together(across, out_following)
    from_following = swap_last(out_following, 1)
    out_across = outputs(across)
    from_following, out_across, blocks = together(from_following, out_across, blocks)
    out_across, first_pulse = in_step(out_across)
    for_near = swap_last(out_across, 1)
    own = outputs(blocks, from_following)
    for_near, own, out_near = together(for_near, own, out_near)
    for_near = [add(a, b).astype(jnp.bfloat16) for a, b in zip(out_near, for_near)]
    for_near, pulse = in_step(for_near)
    from_near = swap_last(for_near, 0)
    from_near, own = together(from_near, own)
    from_near, other_pulse = in_step(from_near)
    pulse = 0.0 * (first_pulse + pulse + other_pulse)
    left, got = own, from_near
    for phase, link in ((1, 1), (1, 0), (0, 1), (0, 0)):
        half = left[0].shape[0] // 2
        sent = [add(t[half:], g[half:]).astype(jnp.bfloat16) for t, g in zip(left, got)]
        left = [add(t[:half], g[:half]).astype(jnp.bfloat16) for t, g in zip(left, got)]
        got = [swap(value, order[phase], link) for value, order in zip(sent, ORDERS)]
        left, got = together(left, got)
    update = jnp.concatenate([add(*ts) for ts in zip(left, got)], axis=0)

    final_rows = (hidden_rows.astype(jnp.float32) + update).astype(jnp.bfloat16)
    normed = normalize(final_rows, module_gain + pulse)
    packed = pack_module(normed, accepted, owner_map, owners)
    delivered = lax.all_to_all(packed, "expert", split_axis=0, concat_axis=0, tiled=True)
    return (final_rows, unpack(delivered)[None, None])


def solution(mesh):
    return jax.shard_map(
        body,
        mesh=mesh,
        in_specs=(
            P(("dp", "expert"), None),
            P(("dp", "expert"), None),
            P(("dp", "expert"), None),
            P("expert", None, "dp"),
            P("expert", None, "dp"),
            P("expert", "dp", None),
            P(),
            P(("dp", "expert")),
            P(("dp", "expert")),
        ),
        out_specs=(P(("dp", "expert"), None), P("dp", "expert", None, None, None)),
        check_vma=False,
    )
```
